256 devices in a mesh: rep: 16 (over y, x_hi, core), fsdp: 16 (over x_lo, z).
Axes of the slice: x: 4 (x_hi: 2, x_lo: 2; x = x_hi * 2 + x_lo), y: 4, z: 8, core: 2. Of those that a mesh axis runs over, the one named last changes fastest.
Arguments:
- activations: bfloat16 [16, 4096, 5120], P('rep', 'fsdp'), may hold values from -6 to 6
- key_weights: bfloat16 [16, 5120, 1024], P('rep', 'fsdp'), may hold values from -0.078125 to 0.078125
- key_cotangent: bfloat16 [16, 4096, 1024], P('rep', 'fsdp'), may hold values from -6 to 6
- fragment: bfloat16 [5120, 1024], P('fsdp'), may hold values from -3 to 3
- pseudo_grads: float32 [16, 5120, 1024], P('rep', 'fsdp'), may hold values from -6 to 6
- momentum: float32 [5120, 1024], P('fsdp', 'rep'), may hold values from -6 to 6
Outputs:
- key_out: bfloat16 [16, 4096, 1024], P('rep', 'fsdp')
- act_grad: bfloat16 [16, 4096, 5120], P('rep', 'fsdp')
- weight_grad: bfloat16 [16, 5120, 1024], P('rep', 'fsdp')
- new_fragment: bfloat16 [5120, 1024], P('fsdp')
- new_momentum: float32 [5120, 1024], P('fsdp', 'rep')
The draws below stay inside these ranges and needn't reach their ends.
All inputs are finite; a program needn't handle non-finite values.
Results may differ from the reference program's by a relative error of at most 0.00125.
Values may be sent and summed in bfloat16 or wider, within the bound.
No kernel may reach another device: no remote copies, remote signals or barrier semaphores. Data moves between devices by JAX's collectives and lax.ppermute only.
A program may use at most 128 MiB of HBM per device.

```python
import math
import jax
import jax.numpy as jnp
from jax import lax

D = 5120
KV = 1024
TOK_DEV = 256
TOKENS = 4096
N_REP = 16


def raised(drawn, stream_key, source, target, blocks, factor):
    def block_of(axis_at):
        return (jnp.arange(drawn.shape[axis_at]) // (drawn.shape[axis_at] // blocks)).reshape((-1,) + (1,) * (drawn.ndim - 1 - axis_at))

    near = jax.random.permutation(stream_key, blocks)[block_of(target)]
    far = (block_of(target) + blocks // 2) % blocks
    return jnp.where((block_of(source) == near) | (block_of(source) == far), factor * drawn, drawn)


def steps_of(own_key, shape, pieces, least, top_value):
    factor_of, own = 1.0, jax.random.fold_in(own_key, 6)
    for dim, shards_of in pieces:
        heights = jnp.exp(jax.random.uniform(jax.random.fold_in(own, dim), (shards_of,), jnp.float32, least / len(pieces), top_value / len(pieces)))
        factor_of = factor_of * jnp.repeat(heights, shape[dim] // shards_of).reshape([-1 if axis == dim else 1 for axis in range(len(shape))])
    return factor_of


def gaussian(key, dims, spread, limit, shards=(), dtype=jnp.bfloat16):
    gain = steps_of(key, dims, shards, -0.22, 0.18) if shards else 1.0
    array = jax.random.normal(key, dims, jnp.float32) * spread * gain
    return jnp.minimum(jnp.maximum(array, -limit), limit).astype(dtype)


def bell_draw_with(key, dims, deviation, bound, split, heavy, held_as=jnp.bfloat16):
    array = deviation * jax.random.normal(key, dims, jnp.float32)
    if split:
        array = array * steps_of(key, dims, split, -0.22, 0.18)
    return jnp.clip(raised(array, jax.random.fold_in(key, 3), *heavy), -bound, bound).astype(held_as)


def setup_inputs(seed: int = 0) -> dict:
    key_list = jax.random.split(jax.random.key(seed), 7)
    return {
        "activations": gaussian(key_list[0], (N_REP, TOKENS, D), 1.0, 6.0, ((0, 16), (1, 16))),
        "key_weights": gaussian(key_list[1], (N_REP, D, KV), D ** -0.5, 0.078125, ((0, 16), (1, 16))),
        "key_cotangent": gaussian(key_list[2], (N_REP, TOKENS, KV), 1.0, 6.0, ((0, 16), (1, 16))),
        "fragment": gaussian(key_list[3], (D, KV), 0.5, 3.0, ((0, 16),)),
        "pseudo_grads": bell_draw_with(key_list[4], (N_REP, D, KV), 1.0, 6.0, ((0, 16), (1, 16)), (0, 2, 16, 2.0), jnp.float32),
        "momentum": gaussian(key_list[5], (D, KV), 1.0, 6.0, ((0, 16), (1, 16)), jnp.float32),
    }


OUTER_RATE = 0.7
NESTEROV = 0.9

def replica_work(packed):
    tokens_in, weight_in, cotangent_in = packed
    key_out = jnp.dot(tokens_in, weight_in, preferred_element_type=jnp.float32).astype(jnp.bfloat16)
    act_grad = jnp.dot(cotangent_in, weight_in.T, preferred_element_type=jnp.float32).astype(jnp.bfloat16)
    factor = 1.0 / math.sqrt(TOKENS)
    token_blocks = tokens_in.reshape(TOKENS // TOK_DEV, TOK_DEV, D)
    grad_blocks = cotangent_in.reshape(TOKENS // TOK_DEV, TOK_DEV, KV)

    def accumulate(summed, block):
        tokens_blk, grads_blk = block
        partial_value = jnp.dot(tokens_blk.T, grads_blk, preferred_element_type=jnp.float32) * factor
        return (summed + partial_value, None)
    summed, _ = lax.scan(accumulate, jnp.zeros((D, KV), jnp.float32), (token_blocks, grad_blocks))
    return (key_out, act_grad, summed.astype(jnp.bfloat16))

def reference(activations, key_weights, key_cotangent, fragment, pseudo_grads, momentum):
    key_out, act_grad, weight_grad = lax.map(replica_work, (activations, key_weights, key_cotangent))
    average = lax.optimization_barrier(jnp.sum(pseudo_grads, axis=0)) / N_REP
    new_momentum = NESTEROV * momentum + average
    new_fragment = (fragment.astype(jnp.float32) - OUTER_RATE * (average + NESTEROV * new_momentum)).astype(jnp.bfloat16)
    return (key_out, act_grad, weight_grad, new_fragment, new_momentum)
```

```python
import jax
import jax.numpy as jnp
from jax import lax
from jax.sharding import Mesh
from jax.sharding import PartitionSpec as P

OUTER_RATE = 0.7
NESTEROV = 0.9
BF16 = jnp.bfloat16
F32 = jnp.float32
F16 = jnp.float16

SIZES = {"y": 4, "xh": 2, "c": 2, "xl": 2, "z": 8}
REP = ("y", "xh", "c")
FSDP = ("xl", "z")
N_Z = 8
EVEN = [(i, i ^ 1) for i in range(N_Z)]
ODD = [(i, (i - 1) % N_Z if i % 2 == 0 else (i + 1) % N_Z) for i in range(N_Z)]


def swap(value, axis, mask=1):
    return lax.ppermute(value, axis, [(i, i ^ mask) for i in range(SIZES[axis])])


def rows_of(array, start, size):
    return lax.dynamic_slice_in_dim(array, start, size, 0)


def columns_of(array, start, size):
    return lax.dynamic_slice_in_dim(array, start, size, 1)


def in_order(here, mine, theirs, axis):
    first = here == 0
    return jnp.concatenate(
        [jnp.where(first, mine, theirs), jnp.where(first, theirs, mine)], axis=axis
    )


def encode(scaled):
    return (scaled * jnp.abs(scaled)).astype(F16)


def decode(sent):
    wide = sent.astype(F32)
    return jnp.sign(wide) * jnp.sqrt(jnp.abs(wide))


def link_bound(tokens, cotangent):
    peak_a = jnp.max(jnp.sum(jnp.abs(tokens.astype(F32)), axis=0))
    peak_c = jnp.max(jnp.abs(cotangent)).astype(F32)
    row = lax.broadcasted_iota(jnp.int32, (8, 128), 0)
    peaks = jnp.where(row < 4, peak_a, peak_c)
    for axis, mask in (("xl", 1), ("z", 1), ("z", 2), ("z", 4)):
        other = swap(peaks, axis, mask)
        peaks = jnp.where(row < 4, peaks + other, jnp.maximum(peaks, other))
    return jnp.maximum(peaks[0, 0] * peaks[4, 0], 1e-32)


def reduce_over_z(partial, bound):
    scale = 240.0 / bound
    z = lax.axis_index("z")
    sign = 1 - 2 * (z % 2)
    chunk = partial.shape[0] // N_Z
    half = chunk // 2

    def own(distance, part):
        block = (z + distance) % N_Z
        return rows_of(partial, block * chunk + part * half, half) * scale

    def send(value, pairs):
        return lax.ppermute(encode(value), "z", pairs)

    even = [send(own(4, 0), EVEN), None]
    odd = [None, send(own(4, 1), ODD)]
    for distance in (3, 2, 1):
        next_even, next_odd = [None, None], [None, None]
        for part in (0, 1):
            value = own(sign * distance, part)
            if odd[part] is not None:
                value = value + decode(odd[part])
            next_even[part] = send(value, EVEN)
            value = own(-sign * distance, part)
            if even[part] is not None:
                value = value + decode(even[part])
            next_odd[part] = send(value, ODD)
        even, odd = next_even, next_odd
    back = bound / (64.0 * 240.0)
    parts = [(own(0, p) + decode(even[p]) + decode(odd[p])) * back for p in (0, 1)]
    return jnp.concatenate(parts, axis=0).astype(BF16)


def outer_step(fragment, pseudo, momentum):
    y, xh, c = (lax.axis_index(a) for a in REP)
    rows = pseudo.shape[0] // 2
    width = momentum.shape[1]
    mine, theirs = c * rows, (1 - c) * rows
    total = rows_of(pseudo, mine, rows) + swap(rows_of(pseudo, theirs, rows), "c")
    quarter = 4 * width
    summed = columns_of(total, y * quarter, quarter)
    for mask in (1, 2, 3):
        summed = summed + swap(columns_of(total, (y ^ mask) * quarter, quarter), "y", mask)
    pair = 2 * width
    summed = columns_of(summed, xh * pair, pair) + swap(
        columns_of(summed, (1 - xh) * pair, pair), "xh"
    )
    average = summed / 16
    old = in_order(c, rows_of(momentum, mine, rows), swap(rows_of(momentum, theirs, rows), "c"), 1)
    new = NESTEROV * old + average
    here = lax.dynamic_slice(fragment, (mine, (2 * y + xh) * pair), (rows, pair))
    updated = (here.astype(F32) - OUTER_RATE * (average + NESTEROV * new)).astype(BF16)
    left, right = new[:, :width], new[:, width:]
    keep = jnp.where(c == 0, left, right)
    give = jnp.where(c == 0, right, left)
    new_momentum = in_order(c, keep, swap(give, "c"), 0)
    wide = in_order(xh, updated, swap(updated, "xh"), 1)
    block = jnp.zeros((rows, 4 * quarter), BF16)
    block = lax.dynamic_update_slice(block, wide, (0, y * quarter))
    for mask in (1, 2, 3):
        block = lax.dynamic_update_slice(block, swap(wide, "y", mask), (0, (y ^ mask) * quarter))
    return in_order(c, block, swap(block, "c"), 0), new_momentum


def shards(activations, key_weights, key_cotangent, fragment, pseudo_grads, momentum):
    tokens = activations[0]
    weight = key_weights[0]
    cotangent = key_cotangent[0]
    x = lax.axis_index("xl")
    half = tokens.shape[1] // 2
    weight_half = lax.all_gather(weight, "z", axis=0, tiled=True)
    cotangent_other = swap(cotangent, "xl")
    tokens_other = swap(columns_of(tokens, (1 - x) * half, half), "xl")
    tokens_mine = columns_of(tokens, x * half, half)
    bound = link_bound(tokens, cotangent)
    new_fragment, new_momentum = outer_step(fragment, pseudo_grads[0], momentum)
    partial = lax.dot_general(
        jnp.concatenate([tokens_mine, tokens_other], axis=0),
        jnp.concatenate([cotangent, cotangent_other], axis=0),
        (((0,), (0,)), ((), ())),
        preferred_element_type=F32,
    )
    weight_grad = reduce_over_z(partial, bound)

    def keys(left):
        return jnp.dot(left, weight_half, preferred_element_type=F32)

    def grads(left):
        return lax.dot_general(
            left, weight_half, (((1,), (1,)), ((), ())), preferred_element_type=F32
        ).astype(BF16)

    keys_back = swap(keys(tokens_other), "xl")
    grads_back = swap(grads(cotangent_other), "xl")
    key_out = (keys(tokens_mine) + keys_back).astype(BF16)
    act_grad = in_order(x, grads(cotangent), grads_back, 1)
    return (key_out[None], act_grad[None], weight_grad[None], new_fragment, new_momentum)


def solution(mesh):
    fine = Mesh(mesh.devices.reshape(tuple(SIZES.values())), tuple(SIZES))
    return jax.shard_map(
        shards,
        mesh=fine,
        in_specs=(
            P(REP, FSDP, None),
            P(REP, FSDP, None),
            P(REP, FSDP, None),
            P(FSDP, None),
            P(REP, FSDP, None),
            P(FSDP, REP),
        ),
        out_specs=(
            P(REP, FSDP, None),
            P(REP, FSDP, None),
            P(REP, FSDP, None),
            P(FSDP, None),
            P(FSDP, REP),
        ),
        check_vma=False,
    )
```

```python
import jax
import jax.numpy as jnp
from jax import lax
from jax.sharding import Mesh
from jax.sharding import PartitionSpec as P

OUTER_RATE = 0.7
NESTEROV = 0.9
BF16 = jnp.bfloat16
F32 = jnp.float32
F16 = jnp.float16

SIZES = {"y": 4, "xh": 2, "c": 2, "xl": 2, "z": 8}
REP = ("y", "xh", "c")
FSDP = ("xl", "z")
N_Z = 8
EVEN = [(i, i ^ 1) for i in range(N_Z)]
ODD = [(i, (i - 1) % N_Z if i % 2 == 0 else (i + 1) % N_Z) for i in range(N_Z)]


def swap(value, axis, mask=1):
    return lax.ppermute(value, axis, [(i, i ^ mask) for i in range(SIZES[axis])])


class Sequence:
    def __init__(self):
        self.last = ()

    def step(self, *values):
        held = lax.optimization_barrier((*values, *self.last))[: len(values)]
        return held[0] if len(held) == 1 else held

    def did(self, *values):
        self.last = values


def rows_of(array, start, size):
    return lax.dynamic_slice_in_dim(array, start, size, 0)


def columns_of(array, start, size):
    return lax.dynamic_slice_in_dim(array, start, size, 1)


def in_order(here, mine, theirs, axis):
    first = here == 0
    return jnp.concatenate(
        [jnp.where(first, mine, theirs), jnp.where(first, theirs, mine)], axis=axis
    )


def encode(scaled):
    return (scaled * jnp.abs(scaled)).astype(F16)


def decode(sent):
    wide = sent.astype(F32)
    return jnp.sign(wide) * jnp.sqrt(jnp.abs(wide))


def local_peaks(tokens, cotangent):
    peak_a = jnp.max(jnp.sum(jnp.abs(tokens.astype(F32)), axis=0))
    peak_c = jnp.max(jnp.abs(cotangent)).astype(F32)
    row = lax.broadcasted_iota(jnp.int32, (8, 128), 0)
    return jnp.where(row < 4, peak_a, peak_c)


def join_peaks(peaks, other):
    row = lax.broadcasted_iota(jnp.int32, (8, 128), 0)
    return jnp.where(row < 4, peaks + other, jnp.maximum(peaks, other))


def shards(activations, key_weights, key_cotangent, fragment, pseudo_grads, momentum):
    tokens, weight, cotangent, pseudo = (
        a[0] for a in (activations, key_weights, key_cotangent, pseudo_grads)
    )
    y, xh, c, x, z = (lax.axis_index(a) for a in SIZES)
    order = Sequence()
    half = tokens.shape[1] // 2
    cut = weight.shape[1] * 3 // 4
    rows = pseudo.shape[0] // 2
    mine, theirs = c * rows, (1 - c) * rows
    width = momentum.shape[1]
    pair = 2 * width

    weight_left = lax.all_gather(weight[:, :cut], "z", axis=0, tiled=True)

    give = rows_of(pseudo, theirs, rows)
    order.did(give)
    pseudo_other = swap(give, "c")
    peaks = local_peaks(order.step(tokens), cotangent)
    order.did(peaks)
    peaks_other = swap(peaks, "xl")
    total = rows_of(pseudo, mine, rows) + order.step(pseudo_other)

    def every_other(array, first):
        parts = [columns_of(array, (2 * k + first) * pair, pair) for k in range(4)]
        return jnp.concatenate(parts, axis=1)

    give = every_other(total, 1 - xh)
    order.did(give)
    total_other = swap(give, "xh")
    sent = columns_of(order.step(tokens), (1 - x) * half, half)
    sent = jnp.concatenate([sent, cotangent], axis=1)
    order.did(sent)
    pair_other = swap(sent, "xl")
    peaks = join_peaks(peaks, order.step(peaks_other))
    order.did(peaks)
    peaks_other = swap(peaks, "z", 1)
    old_give = rows_of(order.step(momentum), theirs, rows)
    order.did(old_give)
    old_other = swap(old_give, "c")
    peaks = join_peaks(peaks, order.step(peaks_other))
    order.did(peaks)
    peaks_other = swap(peaks, "z", 2)
    total = every_other(total, xh) + order.step(total_other)
    gives = [columns_of(total, (y ^ m) * pair, pair) for m in (1, 2, 3)]
    order.did(*gives)
    others = [swap(g, "y", m) for g, m in zip(gives, (1, 2, 3))]
    peaks = join_peaks(peaks, order.step(peaks_other))
    order.did(peaks)
    peaks_other = swap(peaks, "z", 4)

    *others, old_other = order.step(*others, old_other)
    summed = columns_of(total, y * pair, pair) + others[0] + others[1] + others[2]
    average = summed / 16
    old = in_order(c, rows_of(momentum, mine, rows), old_other, 1)
    new = NESTEROV * old + average
    here = lax.dynamic_slice(fragment, (mine, (2 * y + xh) * pair), (rows, pair))
    updated = (here.astype(F32) - OUTER_RATE * (average + NESTEROV * new)).astype(BF16)
    keep = jnp.where(c == 0, new[:, :width], new[:, width:])
    give = jnp.where(c == 0, new[:, width:], new[:, :width])
    order.did(updated, keep, give)
    updates = [swap(updated, "y", m) for m in (1, 2, 3)]
    new_other = swap(give, "c")
    weight_right = lax.all_gather(order.step(weight)[:, cut:], "z", axis=0, tiled=True)
    peaks = join_peaks(peaks, order.step(peaks_other))
    bound = jnp.maximum(peaks[0, 0] * peaks[4, 0], 1e-32)
    scale, back = 240.0 / bound, bound / (64.0 * 240.0)
    tokens_mine = columns_of(tokens, x * half, half)
    order.did(scale, back, tokens_mine)
    *updates, new_other = order.step(*updates, new_other)
    new_momentum = in_order(c, keep, new_other, 0)
    wide = jnp.zeros((rows, 4 * pair), BF16)
    wide = lax.dynamic_update_slice(wide, updated, (0, y * pair))
    for got, m in zip(updates, (1, 2, 3)):
        wide = lax.dynamic_update_slice(wide, got, (0, (y ^ m) * pair))
    order.did(wide, new_momentum)
    wide_other = swap(wide, "xh")

    pair_other = order.step(pair_other)
    tokens_other, cotangent_other = pair_other[:, :half], pair_other[:, half:]
    partial = lax.dot_general(
        jnp.concatenate([tokens_mine, tokens_other], axis=0),
        jnp.concatenate([cotangent, cotangent_other], axis=0),
        (((0,), (0,)), ((), ())),
        preferred_element_type=F32,
    )
    order.did(partial)
    chunk = partial.shape[0] // N_Z
    part = chunk // 2
    sign = 1 - 2 * (z % 2)

    def own(distance, start=0, size=chunk):
        return rows_of(partial, (z + N_Z + distance) % N_Z * chunk + start, size) * scale

    def send(even, odd):
        even, odd = encode(even), encode(odd)
        order.did(even, odd)
        return lax.ppermute(even, "z", EVEN), lax.ppermute(odd, "z", ODD)

    def ring_step(distance, got):
        even_in, odd_in = order.step(*got)
        return send(own(sign * distance) + decode(odd_in), own(-sign * distance) + decode(even_in))

    def keys(left, right):
        return jnp.dot(left, right, preferred_element_type=F32)

    def grads(left, right):
        return lax.dot_general(left, right, (((1,), (1,)), ((), ())), preferred_element_type=F32)

    far = send(own(4, 0, part), own(4, part, part))

    weight_left = order.step(weight_left)
    keys_left = keys(tokens_other, weight_left)
    grads_left = grads(cotangent_other[:, :cut], weight_left)
    order.did(keys_left, grads_left)
    keys_left_back = swap(keys_left, "xl")

    even_in, odd_in = order.step(*far)
    even = jnp.concatenate([own(3 * sign, 0, part), own(3 * sign, part, part) + decode(odd_in)])
    odd = jnp.concatenate([own(-3 * sign, 0, part) + decode(even_in), own(-3 * sign, part, part)])
    ring = send(even, odd)

    wide_other = order.step(wide_other)
    first = jnp.where(xh == 0, wide, wide_other)
    second = jnp.where(xh == 0, wide_other, wide)
    block = jnp.concatenate(
        [side[:, k * pair : (k + 1) * pair] for k in range(4) for side in (first, second)], axis=1
    )
    order.did(block)
    block_other = swap(block, "c")

    weight_right = order.step(weight_right)
    keys_right = keys(tokens_other, weight_right)
    grads_other = (grads_left + grads(cotangent_other[:, cut:], weight_right)).astype(BF16)
    order.did(keys_right, grads_other)
    grads_back = swap(grads_other, "xl")
    keys_right_back = swap(keys_right, "xl")

    key_left = (keys(tokens_mine, weight_left) + order.step(keys_left_back)).astype(BF16)
    order.did(key_left)
    ring = ring_step(2, ring)
    new_fragment = in_order(c, block, order.step(block_other), 0)
    key_right = keys(tokens_mine, weight_right)
    grads_mine = grads(cotangent[:, :cut], weight_left)
    grads_mine = (grads_mine + grads(cotangent[:, cut:], weight_right)).astype(BF16)
    order.did(new_fragment, key_right, grads_mine)
    ring = ring_step(1, ring)
    even_in, odd_in = order.step(*ring)
    weight_grad = ((own(0) + decode(even_in) + decode(odd_in)) * back).astype(BF16)
    order.did(weight_grad)
    keys_right_back, grads_back = order.step(keys_right_back, grads_back)
    key_right = (key_right + keys_right_back).astype(BF16)
    return (
        jnp.concatenate([key_left, key_right], axis=1)[None],
        in_order(x, grads_mine, grads_back, 1)[None],
        weight_grad[None],
        new_fragment,
        new_momentum,
    )


def solution(mesh):
    fine = Mesh(mesh.devices.reshape(tuple(SIZES.values())), tuple(SIZES))
    return jax.shard_map(
        shards,
        mesh=fine,
        in_specs=(
            P(REP, FSDP, None),
            P(REP, FSDP, None),
            P(REP, FSDP, None),
            P(FSDP, None),
            P(REP, FSDP, None),
            P(FSDP, REP),
        ),
        out_specs=(
            P(REP, FSDP, None),
            P(REP, FSDP, None),
            P(REP, FSDP, None),
            P(FSDP, None),
            P(FSDP, REP),
        ),
        check_vma=False,
    )
```

```python
import jax
import jax.numpy as jnp
from jax import lax
from jax.experimental import pallas as pl
from jax.experimental.pallas import tpu as pltpu
from jax.sharding import Mesh
from jax.sharding import PartitionSpec as P

OUTER_RATE = 0.7
NESTEROV = 0.9
BF16 = jnp.bfloat16
F32 = jnp.float32
F16 = jnp.float16

SIZES = {"y": 4, "xh": 2, "c": 2, "xl": 2, "z": 8}
REP = ("y", "xh", "c")
FSDP = ("xl", "z")
N_Z = 8
EVEN = [(i, i ^ 1) for i in range(N_Z)]
ODD = [(i, (i - 1) % N_Z if i % 2 == 0 else (i + 1) % N_Z) for i in range(N_Z)]


def swap(value, axis, mask=1):
    return lax.ppermute(value, axis, [(i, i ^ mask) for i in range(SIZES[axis])])


class Sequence:
    def __init__(self):
        self.last = ()

    def step(self, *values):
        held = lax.optimization_barrier((*values, *self.last))[: len(values)]
        return held[0] if len(held) == 1 else held

    def did(self, *values):
        self.last = values


def rows_of(array, start, size):
    return lax.dynamic_slice_in_dim(array, start, size, 0)


def columns_of(array, start, size):
    return lax.dynamic_slice_in_dim(array, start, size, 1)


def in_order(here, mine, theirs, axis):
    first = here == 0
    return jnp.concatenate(
        [jnp.where(first, mine, theirs), jnp.where(first, theirs, mine)], axis=axis
    )


def encode(scaled):
    return (scaled * jnp.abs(scaled)).astype(F16)


def decode(sent):
    wide = sent.astype(F32)
    return jnp.sign(wide) * jnp.sqrt(jnp.abs(wide))


def column_peak(tokens):
    return jnp.max(jnp.sum(jnp.abs(tokens.astype(F32)), axis=0))


def as_tile(first, second):
    row = lax.broadcasted_iota(jnp.int32, (8, 128), 0)
    return jnp.where(row < 4, first, second)


def join_peaks(peaks, other):
    return as_tile(peaks + other, jnp.maximum(peaks, other))


def dot(left, right):
    return jnp.dot(left, right, preferred_element_type=F32)


def dot_t(left, right):
    return lax.dot_general(left, right, (((1,), (1,)), ((), ())), preferred_element_type=F32)


FREE = pl.CostEstimate(flops=0, bytes_accessed=0, transcendentals=0)
STEP = 512


def whole(array):
    return pl.BlockSpec(array.shape, lambda i, *_: (0, 0))


def rows_block(array):
    return pl.BlockSpec((STEP, array.shape[1]), lambda i, *_: (i, 0))


def columns_block(array):
    return pl.BlockSpec((array.shape[0], STEP), lambda i, *_: (0, i))


def key_part(tokens, weight):
    def body(tokens_ref, weight_ref, keys_ref):
        @pl.when(pl.program_id(0) == 0)
        def _():
            keys_ref[...] = jnp.zeros_like(keys_ref)

        keys_ref[...] += dot(tokens_ref[...], weight_ref[...])

    shape = (tokens.shape[0], weight.shape[1])
    return pl.pallas_call(
        body,
        grid=(tokens.shape[1] // STEP,),
        in_specs=[columns_block(tokens), rows_block(weight)],
        out_specs=pl.BlockSpec(shape, lambda i: (0, 0)),
        out_shape=jax.ShapeDtypeStruct(shape, F32),
        cost_estimate=FREE,
    )(tokens, weight)


def products_for_partner(tokens, cotangent, left, right):
    cut = left.shape[1]

    def body(tokens_ref, cotangent_ref, left_ref, right_ref, keys_ref, grads_ref):
        @pl.when(pl.program_id(0) == 0)
        def _():
            keys_ref[...] = jnp.zeros_like(keys_ref)

        keys_ref[...] += dot(tokens_ref[...], right_ref[...])
        grads = dot_t(cotangent_ref[:, :cut], left_ref[...])
        grads_ref[...] = (grads + dot_t(cotangent_ref[:, cut:], right_ref[...])).astype(BF16)

    keys = jax.ShapeDtypeStruct((tokens.shape[0], right.shape[1]), F32)
    return pl.pallas_call(
        body,
        grid=(tokens.shape[1] // STEP,),
        in_specs=[columns_block(tokens), whole(cotangent), rows_block(left), rows_block(right)],
        out_specs=[whole(keys), columns_block(tokens)],
        out_shape=[keys, jax.ShapeDtypeStruct(tokens.shape, BF16)],
        cost_estimate=FREE,
    )(tokens, cotangent, left, right)


def products_here(side, tokens, cotangent, left, right):
    cut = left.shape[1]
    steps = left.shape[0] // STEP

    def body(_, tokens_ref, cotangent_ref, left_ref, right_ref, keys_ref, grads_ref):
        @pl.when(pl.program_id(0) == 0)
        def _():
            keys_ref[...] = jnp.zeros_like(keys_ref)

        keys_ref[:, :cut] += dot(tokens_ref[...], left_ref[...])
        keys_ref[:, cut:] += dot(tokens_ref[...], right_ref[...])
        grads = dot_t(cotangent_ref[:, :cut], left_ref[...])
        grads_ref[...] = (grads + dot_t(cotangent_ref[:, cut:], right_ref[...])).astype(BF16)

    keys = jax.ShapeDtypeStruct(cotangent.shape, F32)
    grads = jax.ShapeDtypeStruct(tokens.shape, BF16)
    here = pl.BlockSpec((tokens.shape[0], STEP), lambda i, s: (0, s[0] * steps + i))
    return pl.pallas_call(
        body,
        grid_spec=pltpu.PrefetchScalarGridSpec(
            num_scalar_prefetch=1,
            grid=(steps,),
            in_specs=[here, whole(cotangent), rows_block(left), rows_block(right)],
            out_specs=[whole(keys), here],
        ),
        out_shape=[keys, grads],
        cost_estimate=FREE,
    )(side.reshape(1), tokens, cotangent, left, right)


def fill_other(side, grads, other):
    steps = other.shape[1] // STEP

    def body(_, __, other_ref, out_ref):
        out_ref[...] = other_ref[...]

    return pl.pallas_call(
        body,
        grid_spec=pltpu.PrefetchScalarGridSpec(
            num_scalar_prefetch=1,
            grid=(steps,),
            in_specs=[pl.BlockSpec(memory_space=pl.ANY), columns_block(other)],
            out_specs=pl.BlockSpec(
                (other.shape[0], STEP), lambda i, s: (0, (1 - s[0]) * steps + i)
            ),
        ),
        out_shape=jax.ShapeDtypeStruct(grads.shape, BF16),
        input_output_aliases={1: 0},
    )(side.reshape(1), grads, other)


def shards(activations, key_weights, key_cotangent, fragment, pseudo_grads, momentum):
    tokens, weight, cotangent, pseudo = (
        a[0] for a in (activations, key_weights, key_cotangent, pseudo_grads)
    )
    y, xh, c, x, z = (lax.axis_index(a) for a in SIZES)
    order = Sequence()
    half = tokens.shape[1] // 2
    cut = weight.shape[1] * 3 // 4
    rows = pseudo.shape[0] // 2
    mine, theirs = c * rows, (1 - c) * rows
    width = momentum.shape[1]
    pair = 2 * width
    quarter = 2 * pair
    chunk = half // N_Z
    odd_z = z % 2
    sign = 1 - 2 * odd_z
    group = z // 2
    early = [(group + 2) % 4, (group + 4 + sign) % 4]
    late = [group, (group + 4 - sign) % 4]

    def token_columns(array, side, groups):
        parts = [columns_of(array, side * half + g * 2 * chunk, 2 * chunk) for g in groups]
        return jnp.concatenate(parts, axis=1)

    weight_left = lax.all_gather(weight[:, :cut], "z", axis=0, tiled=True)
    weight_right = lax.all_gather(weight[:, cut:], "z", axis=0, tiled=True)
    cotangent_other = swap(cotangent, "xl")

    give = rows_of(pseudo, theirs, rows)
    order.did(give)
    pseudo_other = swap(give, "c")
    peak = jnp.full((8, 128), column_peak(order.step(tokens)))
    order.did(peak)
    peak_other = swap(peak, "xl")
    sent = token_columns(order.step(tokens), 1 - x, early)
    order.did(sent)
    early_other = swap(sent, "xl")
    pseudo_other, cotangent_other = order.step(pseudo_other, cotangent_other)
    total = rows_of(pseudo, mine, rows) + pseudo_other
    gives = [columns_of(total, (y ^ m) * quarter, quarter) for m in (1, 2, 3)]
    old_give = rows_of(momentum, theirs, rows)
    order.did(*gives, old_give)
    others = [swap(g, "y", m) for g, m in zip(gives, (1, 2, 3))]
    old_other = swap(old_give, "c")
    sent = token_columns(order.step(tokens), 1 - x, late)
    order.did(sent)
    late_other = swap(sent, "xl")
    peak_other = order.step(peak_other)
    peak_c = jnp.maximum(jnp.max(jnp.abs(cotangent)), jnp.max(jnp.abs(cotangent_other)))
    peaks = as_tile(peak + peak_other, peak_c.astype(F32))
    order.did(peaks)
    peaks_other = swap(peaks, "z", 1)
    early_mine = token_columns(order.step(tokens), x, early)
    order.did(early_mine)
    peaks = join_peaks(peaks, order.step(peaks_other))
    order.did(peaks)
    peaks_other = swap(peaks, "z", 2)
    *others, old_other = order.step(*others, old_other)
    summed = columns_of(total, y * quarter, quarter) + others[0] + others[1] + others[2]
    give = columns_of(summed, (1 - xh) * pair, pair)
    order.did(summed, give)
    summed_other = swap(give, "xh")
    peaks = join_peaks(peaks, order.step(peaks_other))
    order.did(peaks)
    peaks_other = swap(peaks, "z", 4)

    def product(first, second):
        return lax.dot_general(
            jnp.concatenate([first, second], axis=0),
            jnp.concatenate([cotangent, cotangent_other], axis=0),
            (((0,), (0,)), ((), ())),
            preferred_element_type=F32,
        )

    early_other = order.step(early_other)
    partial_early = product(early_mine, early_other)
    order.did(partial_early)
    peaks = join_peaks(peaks, order.step(peaks_other))
    bound = jnp.maximum(peaks[0, 0] * peaks[4, 0], 1e-32)
    scale, back = 240.0 / bound, bound / (64.0 * 240.0)
    place = {4: odd_z, -3: 1 - odd_z, 2: 2 + odd_z, 3: 3 - odd_z}
    place_late = {0: odd_z, 1: 1 - odd_z, -2: 2 + odd_z, -1: 3 - odd_z}

    def own(distance, start=0, size=chunk):
        if distance in place:
            return rows_of(partial_early, place[distance] * chunk + start, size) * scale
        return rows_of(partial_late, place_late[distance] * chunk + start, size) * scale

    def send(even, odd):
        even, odd = encode(even), encode(odd)
        order.did(even, odd)
        return lax.ppermute(even, "z", EVEN), lax.ppermute(odd, "z", ODD)

    def ring_step(distance, got):
        even_in, odd_in = order.step(*got)
        return send(own(distance) + decode(odd_in), own(-distance) + decode(even_in))

    part = chunk // 2
    far = send(own(4, 0, part), own(4, part, part))

    late_other = order.step(late_other)
    late_mine = token_columns(tokens, x, late)
    partial_late = product(late_mine, late_other)
    order.did(partial_late)

    even_in, odd_in = order.step(*far)
    even = jnp.concatenate([own(3, 0, part), own(3, part, part) + decode(odd_in)])
    odd = jnp.concatenate([own(-3, 0, part) + decode(even_in), own(-3, part, part)])
    ring = send(even, odd)

    summed_other = order.step(summed_other)
    average = (columns_of(summed, xh * pair, pair) + summed_other) / 16
    old = in_order(c, rows_of(momentum, mine, rows), old_other, 1)
    new = NESTEROV * old + average
    here = lax.dynamic_slice(fragment, (mine, (2 * y + xh) * pair), (rows, pair))
    updated = (here.astype(F32) - OUTER_RATE * (average + NESTEROV * new)).astype(BF16)
    keep = jnp.where(c == 0, new[:, :width], new[:, width:])
    give = jnp.where(c == 0, new[:, width:], new[:, :width])
    order.did(updated, keep, give)
    updated_other = swap(updated, "xh")
    new_other = swap(give, "c")

    tokens_other = jnp.zeros((tokens.shape[0], half), BF16)
    for got, groups in ((order.step(early_other), early), (late_other, late)):
        for k, g in enumerate(groups):
            piece = got[:, k * 2 * chunk : (k + 1) * 2 * chunk]
            tokens_other = lax.dynamic_update_slice(tokens_other, piece, (0, g * 2 * chunk))
    weight_left, tokens_other = lax.optimization_barrier((weight_left, tokens_other))
    keys_left = key_part(tokens_other, weight_left)
    order.did(keys_left)
    keys_left_back = swap(keys_left, "xl")

    updated_other, new_other = order.step(updated_other, new_other)
    new_momentum = in_order(c, keep, new_other, 0)
    wide = in_order(xh, updated, updated_other, 1)
    order.did(wide, new_momentum)
    wides = [swap(wide, "y", m) for m in (1, 2, 3)]

    ring = ring_step(2, ring)

    wides = order.step(*wides)
    block = jnp.zeros((rows, 4 * quarter), BF16)
    block = lax.dynamic_update_slice(block, wide, (0, y * quarter))
    for got, m in zip(wides, (1, 2, 3)):
        block = lax.dynamic_update_slice(block, got, (0, (y ^ m) * quarter))
    order.did(block)
    block_other = swap(block, "c")

    weight_right, keys_left_back = order.step(weight_right, keys_left_back)
    keys_right, grads_other = products_for_partner(
        tokens_other, cotangent_other, weight_left, weight_right
    )
    order.did(keys_right, grads_other)
    grads_back = swap(grads_other, "xl")
    keys_right_back = swap(keys_right, "xl")

    ring = ring_step(1, ring)

    keys_mine, grads_mine = products_here(
        order.step(x), tokens, cotangent, weight_left, weight_right
    )
    order.did(keys_mine, grads_mine)
    new_fragment = in_order(c, block, order.step(block_other), 0)
    key_left = (keys_mine[:, :cut] + keys_left_back).astype(BF16)
    order.did(new_fragment, key_left)
    even_in, odd_in = order.step(*ring)
    weight_grad = ((own(0) + decode(even_in) + decode(odd_in)) * back).astype(BF16)
    order.did(weight_grad)
    keys_right_back, grads_back = order.step(keys_right_back, grads_back)
    key_right = (keys_mine[:, cut:] + keys_right_back).astype(BF16)
    return (
        jnp.concatenate([key_left, key_right], axis=1)[None],
        fill_other(x, grads_mine, grads_back)[None],
        weight_grad[None],
        new_fragment,
        new_momentum,
    )


def solution(mesh):
    fine = Mesh(mesh.devices.reshape(tuple(SIZES.values())), tuple(SIZES))
    return jax.shard_map(
        shards,
        mesh=fine,
        in_specs=(
            P(REP, FSDP, None),
            P(REP, FSDP, None),
            P(REP, FSDP, None),
            P(FSDP, None),
            P(REP, FSDP, None),
            P(FSDP, REP),
        ),
        out_specs=(
            P(REP, FSDP, None),
            P(REP, FSDP, None),
            P(REP, FSDP, None),
            P(FSDP, None),
            P(FSDP, REP),
        ),
        check_vma=False,
    )
```

```python
import jax
import jax.numpy as jnp
from jax import lax
from jax.experimental import pallas as pl
from jax.experimental.pallas import tpu as pltpu
from jax.sharding import Mesh
from jax.sharding import PartitionSpec as P

OUTER_RATE = 0.7
NESTEROV = 0.9
BF16 = jnp.bfloat16
F32 = jnp.float32
F16 = jnp.float16

SIZES = {"y": 4, "xh": 2, "c": 2, "xl": 2, "z": 8}
REP = ("y", "xh", "c")
FSDP = ("xl", "z")
N_Z = 8
EVEN = [(i, i ^ 1) for i in range(N_Z)]
ODD = [(i, (i - 1) % N_Z if i % 2 == 0 else (i + 1) % N_Z) for i in range(N_Z)]


def swap(value, axis, mask=1):
    return lax.ppermute(value, axis, [(i, i ^ mask) for i in range(SIZES[axis])])


class Sequence:
    def __init__(self):
        self.last = ()

    def step(self, *values):
        held = lax.optimization_barrier((*values, *self.last))[: len(values)]
        return held[0] if len(held) == 1 else held

    def did(self, *values):
        self.last = values


def rows_of(array, start, size):
    return lax.dynamic_slice_in_dim(array, start, size, 0)


def columns_of(array, start, size):
    return lax.dynamic_slice_in_dim(array, start, size, 1)


def in_order(here, mine, theirs, axis):
    first = here == 0
    return jnp.concatenate(
        [jnp.where(first, mine, theirs), jnp.where(first, theirs, mine)], axis=axis
    )


def encode(scaled):
    return (scaled * jnp.abs(scaled)).astype(F16)


def decode(sent):
    wide = sent.astype(F32)
    return jnp.sign(wide) * jnp.sqrt(jnp.abs(wide))


def column_peak(tokens):
    return jnp.max(jnp.sum(jnp.abs(tokens.astype(F32)), axis=0))


def as_tile(first, second):
    row = lax.broadcasted_iota(jnp.int32, (8, 128), 0)
    return jnp.where(row < 4, first, second)


def join_peaks(peaks, other):
    return as_tile(peaks + other, jnp.maximum(peaks, other))


def dot(left, right):
    return jnp.dot(left, right, preferred_element_type=F32)


def dot_t(left, right):
    return lax.dot_general(left, right, (((1,), (1,)), ((), ())), preferred_element_type=F32)


FREE = pl.CostEstimate(flops=0, bytes_accessed=0, transcendentals=0)


def whole(array):
    return pl.BlockSpec(array.shape, lambda i, *_: (0, 0))


def assemble(here, places, pieces, axis):
    size = pieces[0].shape[axis]

    def body(here_ref, *refs):
        out_ref = refs[-1]
        for place, piece_ref in zip(places(here_ref[0]), refs[:-1]):
            at = pl.ds(pl.multiple_of(place * size, 32 if axis == 0 else 128), size)
            if axis == 0:
                out_ref[at, :] = piece_ref[...]
            else:
                out_ref[:, at] = piece_ref[...]

    shape = list(pieces[0].shape)
    shape[axis] *= len(pieces)
    out = jax.ShapeDtypeStruct(tuple(shape), pieces[0].dtype)
    return pl.pallas_call(
        body,
        grid_spec=pltpu.PrefetchScalarGridSpec(
            num_scalar_prefetch=1,
            grid=(1,),
            in_specs=[whole(p) for p in pieces],
            out_specs=whole(out),
        ),
        out_shape=out,
        cost_estimate=FREE,
    )(here.reshape(1), *pieces)


def products_for_partner(z, early, late, cotangent, weight):
    count = 4
    wide = weight.shape[0] // count

    def group(i, z_ref):
        step = 1 - 2 * (z_ref[0] % 2)
        return (z_ref[0] // 2 + jnp.where(i % 2 == 1, 4 + step * (2 - i), 2 - i)) % 4

    def body(_, early_ref, late_ref, cotangent_ref, weight_ref, keys_ref, grads_ref):
        i = pl.program_id(0)

        @pl.when(i == 0)
        def _():
            keys_ref[...] = jnp.zeros_like(keys_ref)

        tokens = jnp.where(i < count // 2, early_ref[...], late_ref[...])
        keys_ref[...] += dot(tokens, weight_ref[...])
        grads_ref[...] = dot_t(cotangent_ref[...], weight_ref[...]).astype(BF16)

    rows = cotangent.shape[0]
    keys = jax.ShapeDtypeStruct(cotangent.shape, F32)
    return pl.pallas_call(
        body,
        grid_spec=pltpu.PrefetchScalarGridSpec(
            num_scalar_prefetch=1,
            grid=(count,),
            in_specs=[
                pl.BlockSpec((rows, wide), lambda i, g: (0, jnp.minimum(i, count // 2 - 1))),
                pl.BlockSpec((rows, wide), lambda i, g: (0, jnp.maximum(i - count // 2, 0))),
                whole(cotangent),
                pl.BlockSpec((wide, weight.shape[1]), lambda i, r: (group(i, r), 0)),
            ],
            out_specs=[whole(keys), pl.BlockSpec((rows, wide), lambda i, r: (0, group(i, r)))],
        ),
        out_shape=[keys, jax.ShapeDtypeStruct((rows, weight.shape[0]), BF16)],
        cost_estimate=FREE,
    )(z.reshape(1), early, late, cotangent, weight)


def products_here(side, tokens, cotangent, weight, keys_back):
    count = 4
    wide = weight.shape[0] // count

    def body(_, tokens_ref, cotangent_ref, weight_ref, back_ref, keys_ref, grads_ref, sum_ref):
        @pl.when(pl.program_id(0) == 0)
        def _():
            sum_ref[...] = back_ref[...]

        sum_ref[...] += dot(tokens_ref[...], weight_ref[...])
        grads_ref[...] = dot_t(cotangent_ref[...], weight_ref[...]).astype(BF16)

        @pl.when(pl.program_id(0) == count - 1)
        def _():
            keys_ref[...] = sum_ref[...].astype(BF16)

    keys = jax.ShapeDtypeStruct(cotangent.shape, BF16)
    here = pl.BlockSpec((tokens.shape[0], wide), lambda i, s: (0, s[0] * count + i))
    return pl.pallas_call(
        body,
        grid_spec=pltpu.PrefetchScalarGridSpec(
            num_scalar_prefetch=1,
            grid=(count,),
            in_specs=[
                here,
                whole(cotangent),
                pl.BlockSpec((wide, weight.shape[1]), lambda i, s: (i, 0)),
                whole(keys_back),
            ],
            out_specs=[whole(keys), here],
            scratch_shapes=[pltpu.VMEM(keys_back.shape, F32)],
        ),
        out_shape=[keys, jax.ShapeDtypeStruct(tokens.shape, BF16)],
        cost_estimate=FREE,
    )(side.reshape(1), tokens, cotangent, weight, keys_back)


def shards(activations, key_weights, key_cotangent, fragment, pseudo_grads, momentum):
    tokens, weight, cotangent, pseudo = (
        a[0] for a in (activations, key_weights, key_cotangent, pseudo_grads)
    )
    y, xh, c, x, z = (lax.axis_index(a) for a in SIZES)
    order = Sequence()
    half = tokens.shape[1] // 2
    rows = pseudo.shape[0] // 2
    mine, theirs = c * rows, (1 - c) * rows
    width = momentum.shape[1]
    pair = 2 * width
    quarter = 2 * pair
    chunk = half // N_Z
    odd_z = z % 2
    sign = 1 - 2 * odd_z
    group = z // 2
    early = [(group + 2) % 4, (group + 4 + sign) % 4]
    late = [group, (group + 4 - sign) % 4]

    def token_columns(array, side, groups):
        parts = [columns_of(array, side * half + g * 2 * chunk, 2 * chunk) for g in groups]
        return jnp.concatenate(parts, axis=1)

    weight_half = lax.all_gather(weight, "z", axis=0, tiled=True)
    cotangent_other = swap(cotangent, "xl")

    give = rows_of(pseudo, theirs, rows)
    order.did(give)
    pseudo_other = swap(give, "c")
    peak = jnp.full((8, 128), column_peak(order.step(tokens)))
    order.did(peak)
    peak_other = swap(peak, "xl")
    sent = token_columns(order.step(tokens), 1 - x, early)
    order.did(sent)
    early_other = swap(sent, "xl")
    pseudo_other, cotangent_other = order.step(pseudo_other, cotangent_other)
    total = rows_of(pseudo, mine, rows) + pseudo_other
    gives = [columns_of(total, (y ^ m) * quarter, quarter) for m in (1, 2, 3)]
    old_give = rows_of(momentum, theirs, rows)
    order.did(*gives, old_give)
    others = [swap(g, "y", m) for g, m in zip(gives, (1, 2, 3))]
    old_other = swap(old_give, "c")
    sent = token_columns(order.step(tokens), 1 - x, late)
    order.did(sent)
    late_other = swap(sent, "xl")
    peak_other = order.step(peak_other)
    peak_c = jnp.maximum(jnp.max(jnp.abs(cotangent)), jnp.max(jnp.abs(cotangent_other)))
    peaks = as_tile(peak + peak_other, peak_c.astype(F32))
    order.did(peaks)
    peaks_other = swap(peaks, "z", 1)
    early_mine = token_columns(order.step(tokens), x, early)
    order.did(early_mine)
    peaks = join_peaks(peaks, order.step(peaks_other))
    order.did(peaks)
    peaks_other = swap(peaks, "z", 2)
    *others, old_other = order.step(*others, old_other)
    summed = columns_of(total, y * quarter, quarter) + others[0] + others[1] + others[2]
    give = columns_of(summed, (1 - xh) * pair, pair)
    order.did(summed, give)
    summed_other = swap(give, "xh")
    peaks = join_peaks(peaks, order.step(peaks_other))
    order.did(peaks)
    peaks_other = swap(peaks, "z", 4)

    def product(first, second):
        return lax.dot_general(
            jnp.concatenate([first, second], axis=0),
            jnp.concatenate([cotangent, cotangent_other], axis=0),
            (((0,), (0,)), ((), ())),
            preferred_element_type=F32,
        )

    early_other = order.step(early_other)
    partial_early = product(early_mine, early_other)
    order.did(partial_early)
    peaks = join_peaks(peaks, order.step(peaks_other))
    bound = jnp.maximum(peaks[0, 0] * peaks[4, 0], 1e-32)
    scale, back = 240.0 / bound, bound / (64.0 * 240.0)
    place = {4: odd_z, -3: 1 - odd_z, 2: 2 + odd_z, 3: 3 - odd_z}
    place_late = {0: odd_z, 1: 1 - odd_z, -2: 2 + odd_z, -1: 3 - odd_z}

    def own(distance, start=0, size=chunk):
        if distance in place:
            return rows_of(partial_early, place[distance] * chunk + start, size) * scale
        return rows_of(partial_late, place_late[distance] * chunk + start, size) * scale

    def send(value, pairs):
        message = encode(value)
        order.did(message)
        return lax.ppermute(message, "z", pairs)

    def ring_step(distance, even_in, odd_in):
        odd_out = send(own(-distance) + decode(order.step(even_in)), ODD)
        even_out = send(own(distance) + decode(order.step(odd_in)), EVEN)
        return even_out, odd_out

    part = chunk // 2
    far_even = send(own(4, 0, part), EVEN)
    far_odd = send(own(4, part, part), ODD)

    late_other = order.step(late_other)
    late_mine = token_columns(tokens, x, late)
    partial_late = product(late_mine, late_other)
    order.did(partial_late)

    far_even, far_odd = order.step(far_even, far_odd)
    odd = jnp.concatenate([own(-3, 0, part) + decode(far_even), own(-3, part, part)])
    odd = send(odd, ODD)
    even = jnp.concatenate([own(3, 0, part), own(3, part, part) + decode(far_odd)])
    even = send(even, EVEN)

    summed_other = order.step(summed_other)
    average = (columns_of(summed, xh * pair, pair) + summed_other) / 16
    old = in_order(c, rows_of(momentum, mine, rows), old_other, 1)
    new = NESTEROV * old + average
    here = lax.dynamic_slice(fragment, (mine, (2 * y + xh) * pair), (rows, pair))
    updated = (here.astype(F32) - OUTER_RATE * (average + NESTEROV * new)).astype(BF16)
    keep = jnp.where(c == 0, new[:, :width], new[:, width:])
    give = jnp.where(c == 0, new[:, width:], new[:, :width])
    order.did(updated, keep, give)
    updated_other = swap(updated, "xh")
    new_other = swap(give, "c")

    weight_half = order.step(weight_half)
    keys_other, grads_other = products_for_partner(
        z,
        early_other,
        late_other,
        cotangent_other,
        weight_half,
    )
    order.did(keys_other, grads_other)
    keys_back = swap(keys_other, "xl")
    grads_back = swap(grads_other, "xl")

    updated_other, new_other = order.step(updated_other, new_other)
    new_momentum = assemble(c, lambda i: (i, 1 - i), (keep, new_other), 0)
    wide = assemble(xh, lambda i: (i, 1 - i), (updated, updated_other), 1)
    order.did(wide, new_momentum)
    wides = [swap(wide, "y", m) for m in (1, 2, 3)]

    even, odd = ring_step(2, even, odd)

    wides = order.step(*wides)
    block = assemble(y, lambda i: (i, i ^ 1, i ^ 2, i ^ 3), (wide, *wides), 1)
    order.did(block)
    block_other = swap(block, "c")

    keys_back, even = order.step(keys_back, even)
    even, odd = ring_step(1, even, odd)

    key_out, grads_mine = products_here(
        order.step(x), tokens, cotangent, weight_half, keys_back
    )
    order.did(key_out, grads_mine)
    new_fragment = assemble(c, lambda i: (i, 1 - i), (block, order.step(block_other)), 0)
    order.did(new_fragment)
    even, odd = order.step(even, odd)
    weight_grad = ((own(0) + decode(even) + decode(odd)) * back).astype(BF16)
    order.did(weight_grad)
    act_grad = lax.dynamic_update_slice(grads_mine, order.step(grads_back), (0, (1 - x) * half))
    return (
        key_out[None],
        act_grad[None],
        weight_grad[None],
        new_fragment,
        new_momentum,
    )


def solution(mesh):
    fine = Mesh(mesh.devices.reshape(tuple(SIZES.values())), tuple(SIZES))
    return jax.shard_map(
        shards,
        mesh=fine,
        in_specs=(
            P(REP, FSDP, None),
            P(REP, FSDP, None),
            P(REP, FSDP, None),
            P(FSDP, None),
            P(REP, FSDP, None),
            P(FSDP, REP),
        ),
        out_specs=(
            P(REP, FSDP, None),
            P(REP, FSDP, None),
            P(REP, FSDP, None),
            P(FSDP, None),
            P(FSDP, REP),
        ),
        check_vma=False,
    )
```

```python
import jax
import jax.numpy as jnp
from jax import lax
from jax.experimental import pallas as pl
from jax.experimental.pallas import tpu as pltpu
from jax.sharding import Mesh
from jax.sharding import PartitionSpec as P

OUTER_RATE = 0.7
NESTEROV = 0.9
BF16 = jnp.bfloat16
F32 = jnp.float32
F16 = jnp.float16

SIZES = {"y": 4, "xh": 2, "c": 2, "xl": 2, "z": 8}
REP = ("y", "xh", "c")
FSDP = ("xl", "z")
N_Z = 8
EVEN = [(i, i ^ 1) for i in range(N_Z)]
ODD = [(i, (i - 1) % N_Z if i % 2 == 0 else (i + 1) % N_Z) for i in range(N_Z)]


def swap(value, axis, mask=1):
    return lax.ppermute(value, axis, [(i, i ^ mask) for i in range(SIZES[axis])])


class Sequence:
    def __init__(self):
        self.last = ()

    def step(self, *values):
        held = lax.optimization_barrier((*values, *self.last))[: len(values)]
        return held[0] if len(held) == 1 else held

    def did(self, *values):
        self.last = values


def rows_of(array, start, size):
    return lax.dynamic_slice_in_dim(array, start, size, 0)


def columns_of(array, start, size):
    return lax.dynamic_slice_in_dim(array, start, size, 1)


def in_order(here, mine, theirs, axis):
    first = here == 0
    return jnp.concatenate(
        [jnp.where(first, mine, theirs), jnp.where(first, theirs, mine)], axis=axis
    )


def encode(scaled):
    return (scaled * jnp.abs(scaled)).astype(F16)


def decode(sent):
    wide = sent.astype(F32)
    return jnp.sign(wide) * jnp.sqrt(jnp.abs(wide))


def tile_rows():
    return lax.broadcasted_iota(jnp.int32, (8, 128), 0)


def local_peaks(tokens, cotangent):
    def body(tokens_ref, cotangent_ref, out_ref):
        peak = jnp.max(jnp.sum(jnp.abs(tokens_ref[...].astype(F32)), axis=0, keepdims=True))

        @pl.when(pl.program_id(0) == 0)
        def _():
            other = jnp.max(jnp.abs(cotangent_ref[...].astype(F32)))
            out_ref[...] = jnp.where(tile_rows() < 4, peak, other)

        @pl.when(pl.program_id(0) > 0)
        def _():
            held = out_ref[...]
            out_ref[...] = jnp.where(tile_rows() < 4, jnp.maximum(held, peak), held)

    return pl.pallas_call(
        body,
        grid=(5,),
        in_specs=[
            pl.BlockSpec((tokens.shape[0], tokens.shape[1] // 5), lambda i: (0, i)),
            whole(cotangent),
        ],
        out_specs=pl.BlockSpec((8, 128), lambda i: (0, 0)),
        out_shape=jax.ShapeDtypeStruct((8, 128), F32),
    )(tokens, cotangent)


def join_peaks(peaks, other):
    return jnp.where(tile_rows() < 4, peaks + other, jnp.maximum(peaks, other))


def link_scales(peaks, other):
    def body(peaks_ref, other_ref, out_ref):
        joined = join_peaks(peaks_ref[...], other_ref[...])
        bound = jnp.maximum(joined[:4] * joined[4:], 1e-32)
        out_ref[:4, :] = 240.0 / bound
        out_ref[4:, :] = bound * (1.0 / (64.0 * 240.0))

    return pl.pallas_call(body, out_shape=jax.ShapeDtypeStruct((8, 128), F32))(peaks, other)


def dot(left, right):
    return jnp.dot(left, right, preferred_element_type=F32)


def dot_t(left, right):
    return lax.dot_general(left, right, (((1,), (1,)), ((), ())), preferred_element_type=F32)


FREE = pl.CostEstimate(flops=0, bytes_accessed=0, transcendentals=0)


def whole(array):
    return pl.BlockSpec(array.shape, lambda i, *_: (0, 0))


def assemble(here, places, pieces, axis):
    size = pieces[0].shape[axis]

    def body(here_ref, *refs):
        out_ref = refs[-1]
        for place, piece_ref in zip(places(here_ref[0]), refs[:-1]):
            at = pl.ds(pl.multiple_of(place * size, 32 if axis == 0 else 128), size)
            if axis == 0:
                out_ref[at, :] = piece_ref[...]
            else:
                out_ref[:, at] = piece_ref[...]

    shape = list(pieces[0].shape)
    shape[axis] *= len(pieces)
    out = jax.ShapeDtypeStruct(tuple(shape), pieces[0].dtype)
    return pl.pallas_call(
        body,
        grid_spec=pltpu.PrefetchScalarGridSpec(
            num_scalar_prefetch=1,
            grid=(1,),
            in_specs=[whole(p) for p in pieces],
            out_specs=whole(out),
        ),
        out_shape=out,
        cost_estimate=FREE,
    )(here.reshape(1), *pieces)


TOP = 220.0


def products(z, x, tokens, early, late, cotangent, cotangent_other, weight):
    count = 4
    rows, features = cotangent.shape
    total = weight.shape[0]
    wide = total // count

    def group(i, z_ref):
        step = 1 - 2 * (z_ref[0] % 2)
        return (z_ref[0] // 2 + jnp.where(i % 2 == 1, 4 + step * (2 - i), 2 - i)) % 4

    def body(
        z_ref, _, tokens_ref, early_ref, late_ref, own_ref, other_ref, weight_ref,
        keys_ref, grads_ref, sent_ref, sum_ref, both_ref,
    ):
        i = pl.program_id(0)

        @pl.when(i == 0)
        def _():
            sum_ref[...] = jnp.zeros_like(sum_ref)
            both_ref[:rows, :] = own_ref[...]
            both_ref[rows:, :] = other_ref[...]

        partner = jnp.where(i < count // 2, early_ref[...], late_ref[...])
        sum_ref[...] += dot(jnp.concatenate([tokens_ref[...], partner], axis=0), weight_ref[...])
        grads = dot_t(both_ref[...], weight_ref[...]).astype(BF16)
        grads_ref[...] = grads[:rows]
        place = pl.multiple_of(group(i, z_ref) * wide, 128)
        sent_ref[:rows, pl.ds(place, wide)] = grads[rows:]

        @pl.when(i == count - 1)
        def _():
            keys_ref[...] = sum_ref[:rows, :]
            keys = sum_ref[rows:, :]
            largest = jnp.maximum(jnp.max(jnp.abs(keys)) * 1.01, 1e-30)
            sent = jnp.full((16, features), largest, F32).astype(BF16)
            sent_ref[rows:, :total] = jnp.zeros((16, total), BF16)
            sent_ref[rows:, total:] = sent
            scaled = keys * (TOP / sent[:1, :].astype(F32))
            power = scaled * scaled
            power = power * power
            power = power * power
            power = power * power
            sent_ref[:rows, total:] = jnp.where(scaled < 0, -power, power).astype(BF16)

    columns = tokens.shape[1] // (2 * count)
    mine = pl.BlockSpec((rows, columns), lambda i, z, x: (0, x[0] * count + group(i, z)))
    sent = jax.ShapeDtypeStruct((rows + 16, total + features), BF16)
    return pl.pallas_call(
        body,
        grid_spec=pltpu.PrefetchScalarGridSpec(
            num_scalar_prefetch=2,
            grid=(count,),
            in_specs=[
                mine,
                pl.BlockSpec((rows, wide), lambda i, *_: (0, jnp.minimum(i, count // 2 - 1))),
                pl.BlockSpec((rows, wide), lambda i, *_: (0, jnp.maximum(i - count // 2, 0))),
                whole(cotangent),
                whole(cotangent_other),
                pl.BlockSpec((wide, features), lambda i, z, x: (group(i, z), 0)),
            ],
            out_specs=[
                whole(cotangent),
                mine,
                whole(sent),
            ],
            scratch_shapes=[
                pltpu.VMEM((2 * rows, features), F32),
                pltpu.VMEM((2 * rows, features), BF16),
            ],
        ),
        out_shape=[
            jax.ShapeDtypeStruct(cotangent.shape, F32),
            jax.ShapeDtypeStruct(tokens.shape, BF16),
            sent,
        ],
        compiler_params=pltpu.CompilerParams(vmem_limit_bytes=40 * 1024 * 1024),
        cost_estimate=FREE,
    )(z.reshape(1), x.reshape(1), tokens, early, late, cotangent, cotangent_other, weight)


def decode_keys(coded):
    rows = coded.shape[0] - 16
    power = coded[:rows].astype(F32)
    size = jnp.exp2(jnp.log2(jnp.abs(power)) * (1.0 / 16.0))
    size = jnp.where(power == 0, 0.0, size) * (coded[rows : rows + 1, :1].astype(F32) / TOP)
    return jnp.where(power < 0, -size, size)


def shards(activations, key_weights, key_cotangent, fragment, pseudo_grads, momentum):
    tokens, weight, cotangent, pseudo = (
        a[0] for a in (activations, key_weights, key_cotangent, pseudo_grads)
    )
    y, xh, c, x, z = (lax.axis_index(a) for a in SIZES)
    order = Sequence()
    half = tokens.shape[1] // 2
    rows = pseudo.shape[0] // 2
    mine, theirs = c * rows, (1 - c) * rows
    width = momentum.shape[1]
    pair = 2 * width
    quarter = 2 * pair
    chunk = half // N_Z
    odd_z = z % 2
    sign = 1 - 2 * odd_z
    group = z // 2
    early = [(group + 2) % 4, (group + 4 + sign) % 4]
    late = [group, (group + 4 - sign) % 4]

    def token_columns(array, side, groups):
        parts = [columns_of(array, side * half + g * 2 * chunk, 2 * chunk) for g in groups]
        return jnp.concatenate(parts, axis=1)

    weight_half = lax.all_gather(weight, "z", axis=0, tiled=True)
    cotangent_other = swap(cotangent, "xl")

    give = rows_of(pseudo, theirs, rows)
    order.did(give)
    pseudo_other = swap(give, "c")
    peaks = local_peaks(order.step(tokens), cotangent)
    order.did(peaks)
    peaks_other = swap(peaks, "xl")
    sent = token_columns(order.step(tokens), 1 - x, early)
    order.did(sent)
    early_other = swap(sent, "xl")
    pseudo_other = order.step(pseudo_other)
    total = rows_of(pseudo, mine, rows) + pseudo_other
    gives = [columns_of(total, (y ^ m) * quarter, quarter) for m in (1, 2, 3)]
    old_give = rows_of(momentum, theirs, rows)
    order.did(*gives, old_give)
    others = [swap(g, "y", m) for g, m in zip(gives, (1, 2, 3))]
    old_other = swap(old_give, "c")
    sent = token_columns(order.step(tokens), 1 - x, late)
    order.did(sent)
    late_other = swap(sent, "xl")
    peaks = join_peaks(peaks, order.step(peaks_other))
    order.did(peaks)
    peaks_other = swap(peaks, "z", 1)
    early_mine = token_columns(order.step(tokens), x, early)
    order.did(early_mine)
    peaks = join_peaks(peaks, order.step(peaks_other))
    order.did(peaks)
    peaks_other = swap(peaks, "z", 2)
    *others, old_other = order.step(*others, old_other)
    summed = columns_of(total, y * quarter, quarter) + others[0] + others[1] + others[2]
    give = columns_of(summed, (1 - xh) * pair, pair)
    order.did(summed, give)
    summed_other = swap(give, "xh")
    peaks = join_peaks(peaks, order.step(peaks_other))
    order.did(peaks)
    peaks_other = swap(peaks, "z", 4)

    def product(first, second):
        return lax.dot_general(
            jnp.concatenate([first, second], axis=0),
            jnp.concatenate([cotangent, cotangent_other], axis=0),
            (((0,), (0,)), ((), ())),
            preferred_element_type=F32,
        )

    early_other, cotangent_other = order.step(early_other, cotangent_other)
    partial_early = product(early_mine, early_other)
    order.did(partial_early)
    scales = link_scales(peaks, order.step(peaks_other))
    scale, back = scales[:1, :1], scales[4:5, :1]
    place = {4: odd_z, -3: 1 - odd_z, 2: 2 + odd_z, 3: 3 - odd_z}
    place_late = {0: odd_z, 1: 1 - odd_z, -2: 2 + odd_z, -1: 3 - odd_z}

    def own(distance, start=0, size=chunk):
        if distance in place:
            return rows_of(partial_early, place[distance] * chunk + start, size) * scale
        return rows_of(partial_late, place_late[distance] * chunk + start, size) * scale

    def send(value, pairs):
        message = encode(value)
        order.did(message)
        return lax.ppermute(message, "z", pairs)

    def ring_step(distance, even_in, odd_in):
        odd_out = send(own(-distance) + decode(order.step(even_in)), ODD)
        even_out = send(own(distance) + decode(order.step(odd_in)), EVEN)
        return even_out, odd_out

    part = chunk // 2
    far_even = send(own(4, 0, part), EVEN)
    far_odd = send(own(4, part, part), ODD)

    late_other = order.step(late_other)
    late_mine = token_columns(tokens, x, late)
    partial_late = product(late_mine, late_other)
    order.did(partial_late)

    far_even, far_odd = order.step(far_even, far_odd)
    odd = jnp.concatenate([own(-3, 0, part) + decode(far_even), own(-3, part, part)])
    odd = send(odd, ODD)
    even = jnp.concatenate([own(3, 0, part), own(3, part, part) + decode(far_odd)])
    even = send(even, EVEN)

    summed_other = order.step(summed_other)
    average = (columns_of(summed, xh * pair, pair) + summed_other) / 16
    old = in_order(c, rows_of(momentum, mine, rows), old_other, 1)
    new = NESTEROV * old + average
    here = lax.dynamic_slice(fragment, (mine, (2 * y + xh) * pair), (rows, pair))
    updated = (here.astype(F32) - OUTER_RATE * (average + NESTEROV * new)).astype(BF16)
    keep = jnp.where(c == 0, new[:, :width], new[:, width:])
    give = jnp.where(c == 0, new[:, width:], new[:, :width])
    order.did(updated, keep, give)
    updated_other = swap(updated, "xh")
    new_other = swap(give, "c")

    weight_half = order.step(weight_half)
    keys_mine, grads_mine, sent = products(
        z, x, tokens, early_other, late_other, cotangent, cotangent_other, weight_half
    )
    order.did(sent)
    products_back = swap(sent, "xl")

    updated_other, new_other = order.step(updated_other, new_other)
    new_momentum = assemble(c, lambda i: (i, 1 - i), (keep, new_other), 0)
    wide = assemble(xh, lambda i: (i, 1 - i), (updated, updated_other), 1)
    order.did(wide, new_momentum)
    wides = [swap(wide, "y", m) for m in (1, 2, 3)]

    even, odd = ring_step(2, even, odd)

    wides = order.step(*wides)
    block = assemble(y, lambda i: (i, i ^ 1, i ^ 2, i ^ 3), (wide, *wides), 1)
    order.did(block)
    block_other = swap(block, "c")

    even, odd = order.step(even, odd)
    even, odd = encode(own(1) + decode(odd)), encode(own(-1) + decode(even))
    order.did(even, odd)
    even, odd = lax.ppermute(even, "z", EVEN), lax.ppermute(odd, "z", ODD)

    new_fragment = assemble(c, lambda i: (i, 1 - i), (block, order.step(block_other)), 0)
    order.did(new_fragment)
    even, odd = order.step(even, odd)
    weight_grad = ((own(0) + decode(even) + decode(odd)) * back).astype(BF16)
    order.did(weight_grad)
    products_back = order.step(products_back)
    key_out = (keys_mine + decode_keys(products_back[:, half:])).astype(BF16)
    grads_back = products_back[: tokens.shape[0], :half]
    act_grad = lax.dynamic_update_slice(grads_mine, grads_back, (0, (1 - x) * half))
    return (
        key_out[None],
        act_grad[None],
        weight_grad[None],
        new_fragment,
        new_momentum,
    )


def solution(mesh):
    fine = Mesh(mesh.devices.reshape(tuple(SIZES.values())), tuple(SIZES))
    return jax.shard_map(
        shards,
        mesh=fine,
        in_specs=(
            P(REP, FSDP, None),
            P(REP, FSDP, None),
            P(REP, FSDP, None),
            P(FSDP, None),
            P(REP, FSDP, None),
            P(FSDP, REP),
        ),
        out_specs=(
            P(REP, FSDP, None),
            P(REP, FSDP, None),
            P(REP, FSDP, None),
            P(FSDP, None),
            P(FSDP, REP),
        ),
        check_vma=False,
    )
```

```python
import jax
import jax.numpy as jnp
from jax import lax
from jax.experimental import pallas as pl
from jax.experimental.pallas import tpu as pltpu
from jax.sharding import Mesh
from jax.sharding import PartitionSpec as P

OUTER_RATE = 0.7
NESTEROV = 0.9
BF16 = jnp.bfloat16
F32 = jnp.float32
F16 = jnp.float16

SIZES = {"y": 4, "xh": 2, "c": 2, "xl": 2, "z": 8}
REP = ("y", "xh", "c")
FSDP = ("xl", "z")
N_Z = 8
EVEN = [(i, i ^ 1) for i in range(N_Z)]
ODD = [(i, (i - 1) % N_Z if i % 2 == 0 else (i + 1) % N_Z) for i in range(N_Z)]


def swap(value, axis, mask=1):
    return lax.ppermute(value, axis, [(i, i ^ mask) for i in range(SIZES[axis])])


class Sequence:
    def __init__(self):
        self.last = ()

    def step(self, *values):
        held = lax.optimization_barrier((*values, *self.last))[: len(values)]
        return held[0] if len(held) == 1 else held

    def did(self, *values):
        self.last = values


def rows_of(array, start, size):
    return lax.dynamic_slice_in_dim(array, start, size, 0)


def columns_of(array, start, size):
    return lax.dynamic_slice_in_dim(array, start, size, 1)


def in_order(here, mine, theirs, axis):
    first = here == 0
    return jnp.concatenate(
        [jnp.where(first, mine, theirs), jnp.where(first, theirs, mine)], axis=axis
    )


def encode(scaled):
    return (scaled * jnp.abs(scaled)).astype(F16)


def decode(sent):
    wide = sent.astype(F32)
    return jnp.sign(wide) * jnp.sqrt(jnp.abs(wide))


def tile_rows():
    return lax.broadcasted_iota(jnp.int32, (8, 128), 0)


def local_peaks(tokens, cotangent):
    peak = jnp.max(jnp.sum(jnp.abs(tokens.astype(F32)), axis=0))
    return jnp.where(tile_rows() < 4, peak, jnp.max(jnp.abs(cotangent)).astype(F32))


def join_peaks(peaks, other):
    return jnp.where(tile_rows() < 4, peaks + other, jnp.maximum(peaks, other))


def dot(left, right):
    return jnp.dot(left, right, preferred_element_type=F32)


def dot_t(left, right):
    return lax.dot_general(left, right, (((1,), (1,)), ((), ())), preferred_element_type=F32)


FREE = pl.CostEstimate(flops=0, bytes_accessed=0, transcendentals=0)


def whole(array):
    return pl.BlockSpec(array.shape, lambda i, *_: (0, 0))


def assemble(here, places, pieces, axis):
    size = pieces[0].shape[axis]

    def body(here_ref, *refs):
        out_ref = refs[-1]
        for place, piece_ref in zip(places(here_ref[0]), refs[:-1]):
            at = pl.ds(pl.multiple_of(place * size, 32 if axis == 0 else 128), size)
            if axis == 0:
                out_ref[at, :] = piece_ref[...]
            else:
                out_ref[:, at] = piece_ref[...]

    shape = list(pieces[0].shape)
    shape[axis] *= len(pieces)
    out = jax.ShapeDtypeStruct(tuple(shape), pieces[0].dtype)
    return pl.pallas_call(
        body,
        grid_spec=pltpu.PrefetchScalarGridSpec(
            num_scalar_prefetch=1,
            grid=(1,),
            in_specs=[whole(p) for p in pieces],
            out_specs=whole(out),
        ),
        out_shape=out,
        cost_estimate=FREE,
    )(here.reshape(1), *pieces)


TOP = 220.0


def products_for_partner(z, early, late, cotangent, weight):
    count = 4
    rows, features = cotangent.shape
    wide = weight.shape[0] // count

    def group(i, z_ref):
        step = 1 - 2 * (z_ref[0] % 2)
        return (z_ref[0] // 2 + jnp.where(i % 2 == 1, 4 + step * (2 - i), 2 - i)) % 4

    def body(z_ref, early_ref, late_ref, cotangent_ref, weight_ref, sent_ref, keys_ref):
        i = pl.program_id(0)

        @pl.when(i == 0)
        def _():
            keys_ref[...] = jnp.zeros_like(keys_ref)

        tokens = jnp.where(i < count // 2, early_ref[...], late_ref[...])
        keys_ref[...] += dot(tokens, weight_ref[...])
        place = pl.multiple_of(features + group(i, z_ref) * wide, 128)
        grads = dot_t(cotangent_ref[...], weight_ref[...]).astype(BF16)
        sent_ref[:rows, pl.ds(place, wide)] = grads

        @pl.when(i == count - 1)
        def _():
            keys = keys_ref[...]
            largest = jnp.maximum(jnp.max(jnp.abs(keys)) * 1.01, 1e-30)
            sent = jnp.full((16, features), largest, F32).astype(BF16)
            sent_ref[rows:, :features] = sent
            sent_ref[rows:, features:] = jnp.zeros((16, weight.shape[0]), BF16)
            scaled = keys * (TOP / sent[:1, :].astype(F32))
            power = scaled * scaled
            power = power * power
            power = power * power
            power = power * power
            sent_ref[:rows, :features] = jnp.where(scaled < 0, -power, power).astype(BF16)

    sent = jax.ShapeDtypeStruct((rows + 16, features + weight.shape[0]), BF16)
    return pl.pallas_call(
        body,
        grid_spec=pltpu.PrefetchScalarGridSpec(
            num_scalar_prefetch=1,
            grid=(count,),
            in_specs=[
                pl.BlockSpec((rows, wide), lambda i, z: (0, jnp.minimum(i, count // 2 - 1))),
                pl.BlockSpec((rows, wide), lambda i, z: (0, jnp.maximum(i - count // 2, 0))),
                whole(cotangent),
                pl.BlockSpec((wide, features), lambda i, z: (group(i, z), 0)),
            ],
            out_specs=whole(sent),
            scratch_shapes=[pltpu.VMEM(cotangent.shape, F32)],
        ),
        out_shape=sent,
        cost_estimate=FREE,
    )(z.reshape(1), early, late, cotangent, weight)


def products_here(x, tokens, cotangent, weight, back):
    count = 5
    rows, features = cotangent.shape
    wide = weight.shape[0] // count

    def body(
        _, tokens_ref, cotangent_ref, weight_ref, coded_ref, back_ref, keys_ref, grads_ref, sum_ref
    ):
        i = pl.program_id(0)

        @pl.when(i == 0)
        def _():
            power = coded_ref[:rows, :].astype(F32)
            size = jnp.exp2(jnp.log2(jnp.abs(power)) * (1.0 / 16.0))
            size = jnp.where(power == 0, 0.0, size) * (coded_ref[rows:, :].astype(F32)[:1] / TOP)
            sum_ref[...] = jnp.where(power < 0, -size, size)

        @pl.when(i < count)
        def _():
            sum_ref[...] += dot(tokens_ref[...], weight_ref[...])
            grads_ref[...] = dot_t(cotangent_ref[...], weight_ref[...]).astype(BF16)

        @pl.when(i >= count)
        def _():
            grads_ref[...] = back_ref[...]

        @pl.when(i == count - 1)
        def _():
            keys_ref[...] = sum_ref[...].astype(BF16)

    def block(i):
        return jnp.minimum(i, count - 1)

    return pl.pallas_call(
        body,
        grid_spec=pltpu.PrefetchScalarGridSpec(
            num_scalar_prefetch=1,
            grid=(2 * count,),
            in_specs=[
                pl.BlockSpec((rows, wide), lambda i, x: (0, x[0] * count + block(i))),
                whole(cotangent),
                pl.BlockSpec((wide, features), lambda i, x: (block(i), 0)),
                pl.BlockSpec((rows + 16, features), lambda i, x: (0, 0)),
                pl.BlockSpec(
                    (rows, wide), lambda i, x: (0, features // wide + jnp.maximum(i - count, 0))
                ),
            ],
            out_specs=[
                whole(cotangent),
                pl.BlockSpec((rows, wide), lambda i, x: (0, (x[0] * count + i) % (2 * count))),
            ],
            scratch_shapes=[pltpu.VMEM(cotangent.shape, F32)],
        ),
        out_shape=[
            jax.ShapeDtypeStruct(cotangent.shape, BF16),
            jax.ShapeDtypeStruct(tokens.shape, BF16),
        ],
        cost_estimate=FREE,
    )(x.reshape(1), tokens, cotangent, weight, back, back)


def shards(activations, key_weights, key_cotangent, fragment, pseudo_grads, momentum):
    tokens, weight, cotangent, pseudo = (
        a[0] for a in (activations, key_weights, key_cotangent, pseudo_grads)
    )
    y, xh, c, x, z = (lax.axis_index(a) for a in SIZES)
    order = Sequence()
    half = tokens.shape[1] // 2
    rows = pseudo.shape[0] // 2
    mine, theirs = c * rows, (1 - c) * rows
    width = momentum.shape[1]
    pair = 2 * width
    quarter = 2 * pair
    chunk = half // N_Z
    odd_z = z % 2
    sign = 1 - 2 * odd_z
    group = z // 2
    early = [(group + 2) % 4, (group + 4 + sign) % 4]
    late = [group, (group + 4 - sign) % 4]

    def token_columns(array, side, groups):
        parts = [columns_of(array, side * half + g * 2 * chunk, 2 * chunk) for g in groups]
        return jnp.concatenate(parts, axis=1)

    weight_half = lax.all_gather(weight, "z", axis=0, tiled=True)
    cotangent_other = swap(cotangent, "xl")

    give = rows_of(pseudo, theirs, rows)
    order.did(give)
    pseudo_other = swap(give, "c")
    peaks = local_peaks(order.step(tokens), cotangent)
    order.did(peaks)
    peaks_other = swap(peaks, "xl")
    sent = token_columns(order.step(tokens), 1 - x, early)
    order.did(sent)
    early_other = swap(sent, "xl")
    pseudo_other = order.step(pseudo_other)
    total = rows_of(pseudo, mine, rows) + pseudo_other
    gives = [columns_of(total, (y ^ m) * quarter, quarter) for m in (1, 2, 3)]
    old_give = rows_of(momentum, theirs, rows)
    order.did(*gives, old_give)
    others = [swap(g, "y", m) for g, m in zip(gives, (1, 2, 3))]
    old_other = swap(old_give, "c")
    tokens_held, cotangent_other = order.step(tokens, cotangent_other)
    sent = token_columns(tokens_held, 1 - x, late)
    order.did(sent)
    late_other = swap(sent, "xl")
    peaks = join_peaks(peaks, order.step(peaks_other))
    order.did(peaks)
    peaks_other = swap(peaks, "z", 1)
    early_mine = token_columns(order.step(tokens), x, early)
    order.did(early_mine)
    peaks = join_peaks(peaks, order.step(peaks_other))
    order.did(peaks)
    peaks_other = swap(peaks, "z", 2)
    *others, old_other = order.step(*others, old_other)
    summed = columns_of(total, y * quarter, quarter) + others[0] + others[1] + others[2]
    give = columns_of(summed, (1 - xh) * pair, pair)
    order.did(summed, give)
    summed_other = swap(give, "xh")
    peaks = join_peaks(peaks, order.step(peaks_other))
    order.did(peaks)
    peaks_other = swap(peaks, "z", 4)

    def product(first, second):
        return lax.dot_general(
            jnp.concatenate([first, second], axis=0),
            jnp.concatenate([cotangent, cotangent_other], axis=0),
            (((0,), (0,)), ((), ())),
            preferred_element_type=F32,
        )

    early_other = order.step(early_other)
    partial_early = product(early_mine, early_other)
    order.did(partial_early)
    peaks = join_peaks(peaks, order.step(peaks_other))
    bound = jnp.maximum(peaks[0, 0] * peaks[4, 0], 1e-32)
    scale, back = 240.0 / bound, bound / (64.0 * 240.0)
    place = {4: odd_z, -3: 1 - odd_z, 2: 2 + odd_z, 3: 3 - odd_z}
    place_late = {0: odd_z, 1: 1 - odd_z, -2: 2 + odd_z, -1: 3 - odd_z}

    def own(distance, start=0, size=chunk):
        if distance in place:
            return rows_of(partial_early, place[distance] * chunk + start, size) * scale
        return rows_of(partial_late, place_late[distance] * chunk + start, size) * scale

    def send(value, pairs):
        message = encode(value)
        order.did(message)
        return lax.ppermute(message, "z", pairs)

    def ring_step(distance, even_in, odd_in):
        odd_out = send(own(-distance) + decode(order.step(even_in)), ODD)
        even_out = send(own(distance) + decode(order.step(odd_in)), EVEN)
        return even_out, odd_out

    part = chunk // 2
    far_even = send(own(4, 0, part), EVEN)
    far_odd = send(own(4, part, part), ODD)

    late_other = order.step(late_other)
    late_mine = token_columns(tokens, x, late)
    partial_late = product(late_mine, late_other)
    order.did(partial_late)

    summed_other = order.step(summed_other)
    average = (columns_of(summed, xh * pair, pair) + summed_other) / 16
    old = in_order(c, rows_of(momentum, mine, rows), old_other, 1)
    new = NESTEROV * old + average
    here = lax.dynamic_slice(fragment, (mine, (2 * y + xh) * pair), (rows, pair))
    updated = (here.astype(F32) - OUTER_RATE * (average + NESTEROV * new)).astype(BF16)
    keep = jnp.where(c == 0, new[:, :width], new[:, width:])
    give = jnp.where(c == 0, new[:, width:], new[:, :width])
    order.did(updated, keep, give)
    updated_other = swap(updated, "xh")
    new_other = swap(give, "c")

    far_even, far_odd = order.step(far_even, far_odd)
    odd = jnp.concatenate([own(-3, 0, part) + decode(far_even), own(-3, part, part)])
    odd = send(odd, ODD)
    even = jnp.concatenate([own(3, 0, part), own(3, part, part) + decode(far_odd)])
    even = send(even, EVEN)

    updated_other = order.step(updated_other)
    wide = assemble(xh, lambda i: (i, 1 - i), (updated, updated_other), 1)
    order.did(wide)
    wides = [swap(wide, "y", m) for m in (1, 2, 3)]

    weight_half = order.step(weight_half)
    sent = products_for_partner(z, early_other, late_other, cotangent_other, weight_half)
    order.did(sent)
    products_back = swap(sent, "xl")

    even, odd = ring_step(2, even, odd)

    wides = order.step(*wides)
    block = assemble(y, lambda i: (i, i ^ 1, i ^ 2, i ^ 3), (wide, *wides), 1)
    order.did(block)
    block_other = swap(block, "c")

    even, odd = order.step(even, odd)
    even, odd = encode(own(1) + decode(odd)), encode(own(-1) + decode(even))
    order.did(even, odd)
    even, odd = lax.ppermute(even, "z", EVEN), lax.ppermute(odd, "z", ODD)

    new_momentum = assemble(c, lambda i: (i, 1 - i), (keep, order.step(new_other)), 0)
    order.did(new_momentum)
    new_fragment = assemble(c, lambda i: (i, 1 - i), (block, order.step(block_other)), 0)
    order.did(new_fragment)
    key_out, act_grad = products_here(
        x, tokens, cotangent, weight_half, order.step(products_back)
    )
    order.did(key_out, act_grad)
    even, odd = order.step(even, odd)
    weight_grad = ((own(0) + decode(even) + decode(odd)) * back).astype(BF16)
    order.did(weight_grad)
    return (
        key_out[None],
        act_grad[None],
        weight_grad[None],
        new_fragment,
        new_momentum,
    )


def solution(mesh):
    fine = Mesh(mesh.devices.reshape(tuple(SIZES.values())), tuple(SIZES))
    return jax.shard_map(
        shards,
        mesh=fine,
        in_specs=(
            P(REP, FSDP, None),
            P(REP, FSDP, None),
            P(REP, FSDP, None),
            P(FSDP, None),
            P(REP, FSDP, None),
            P(FSDP, REP),
        ),
        out_specs=(
            P(REP, FSDP, None),
            P(REP, FSDP, None),
            P(REP, FSDP, None),
            P(FSDP, None),
            P(FSDP, REP),
        ),
        check_vma=False,
    )
```

```python
import jax
import jax.numpy as jnp
from jax import lax
from jax.experimental import pallas as pl
from jax.experimental.pallas import tpu as pltpu
from jax.sharding import Mesh
from jax.sharding import PartitionSpec as P

OUTER_RATE = 0.7
NESTEROV = 0.9
BF16 = jnp.bfloat16
F32 = jnp.float32
F16 = jnp.float16

SIZES = {"y": 4, "xh": 2, "c": 2, "xl": 2, "z": 8}
REP = ("y", "xh", "c")
FSDP = ("xl", "z")
N_Z = 8
EVEN = [(i, i ^ 1) for i in range(N_Z)]
ODD = [(i, (i - 1) % N_Z if i % 2 == 0 else (i + 1) % N_Z) for i in range(N_Z)]


def swap(value, axis, mask=1):
    return lax.ppermute(value, axis, [(i, i ^ mask) for i in range(SIZES[axis])])


class Sequence:
    def __init__(self):
        self.last = ()

    def step(self, *values):
        held = lax.optimization_barrier((*values, *self.last))[: len(values)]
        return held[0] if len(held) == 1 else held

    def did(self, *values):
        self.last = values


def rows_of(array, start, size):
    return lax.dynamic_slice_in_dim(array, start, size, 0)


def columns_of(array, start, size):
    return lax.dynamic_slice_in_dim(array, start, size, 1)


def in_order(here, mine, theirs, axis):
    first = here == 0
    return jnp.concatenate(
        [jnp.where(first, mine, theirs), jnp.where(first, theirs, mine)], axis=axis
    )


def encode(scaled):
    return (scaled * jnp.abs(scaled)).astype(F16)


def decode(sent):
    wide = sent.astype(F32)
    return jnp.sign(wide) * jnp.sqrt(jnp.abs(wide))


def tile_rows():
    return lax.broadcasted_iota(jnp.int32, (8, 128), 0)


def local_peaks(tokens, cotangent):
    peak = jnp.max(jnp.sum(jnp.abs(tokens.astype(F32)), axis=0))
    return jnp.where(tile_rows() < 4, peak, jnp.max(jnp.abs(cotangent)).astype(F32))


def join_peaks(peaks, other):
    return jnp.where(tile_rows() < 4, peaks + other, jnp.maximum(peaks, other))


def dot(left, right):
    return jnp.dot(left, right, preferred_element_type=F32)


def dot_t(left, right):
    return lax.dot_general(left, right, (((1,), (1,)), ((), ())), preferred_element_type=F32)


FREE = pl.CostEstimate(flops=0, bytes_accessed=0, transcendentals=0)


def whole(array):
    return pl.BlockSpec(array.shape, lambda i, *_: (0, 0))


def assemble(here, places, pieces, axis):
    size = pieces[0].shape[axis]

    def body(here_ref, *refs):
        out_ref = refs[-1]
        for place, piece_ref in zip(places(here_ref[0]), refs[:-1]):
            at = pl.ds(pl.multiple_of(place * size, 32 if axis == 0 else 128), size)
            if axis == 0:
                out_ref[at, :] = piece_ref[...]
            else:
                out_ref[:, at] = piece_ref[...]

    shape = list(pieces[0].shape)
    shape[axis] *= len(pieces)
    out = jax.ShapeDtypeStruct(tuple(shape), pieces[0].dtype)
    return pl.pallas_call(
        body,
        grid_spec=pltpu.PrefetchScalarGridSpec(
            num_scalar_prefetch=1,
            grid=(1,),
            in_specs=[whole(p) for p in pieces],
            out_specs=whole(out),
        ),
        out_shape=out,
        cost_estimate=FREE,
    )(here.reshape(1), *pieces)


TOP = 220.0


def products_for_partner(z, early, late, cotangent, weight):
    count = 4
    rows, features = cotangent.shape
    wide = weight.shape[0] // count

    def group(i, z_ref):
        step = 1 - 2 * (z_ref[0] % 2)
        return (z_ref[0] // 2 + jnp.where(i % 2 == 1, 4 + step * (2 - i), 2 - i)) % 4

    def body(z_ref, early_ref, late_ref, cotangent_ref, weight_ref, sent_ref, keys_ref):
        i = pl.program_id(0)

        @pl.when(i == 0)
        def _():
            keys_ref[...] = jnp.zeros_like(keys_ref)

        tokens = jnp.where(i < count // 2, early_ref[...], late_ref[...])
        keys_ref[...] += dot(tokens, weight_ref[...])
        place = pl.multiple_of(features + group(i, z_ref) * wide, 128)
        grads = dot_t(cotangent_ref[...], weight_ref[...]).astype(BF16)
        sent_ref[:rows, pl.ds(place, wide)] = grads

        @pl.when(i == count - 1)
        def _():
            keys = keys_ref[...]
            largest = jnp.maximum(jnp.max(jnp.abs(keys)) * 1.01, 1e-30)
            sent = jnp.full((16, features), largest, F32).astype(BF16)
            sent_ref[rows:, :features] = sent
            sent_ref[rows:, features:] = jnp.zeros((16, weight.shape[0]), BF16)
            scaled = keys * (TOP / sent[:1, :].astype(F32))
            power = scaled * scaled
            power = power * power
            power = power * power
            power = power * power
            sent_ref[:rows, :features] = jnp.where(scaled < 0, -power, power).astype(BF16)

    sent = jax.ShapeDtypeStruct((rows + 16, features + weight.shape[0]), BF16)
    return pl.pallas_call(
        body,
        grid_spec=pltpu.PrefetchScalarGridSpec(
            num_scalar_prefetch=1,
            grid=(count,),
            in_specs=[
                pl.BlockSpec((rows, wide), lambda i, z: (0, jnp.minimum(i, count // 2 - 1))),
                pl.BlockSpec((rows, wide), lambda i, z: (0, jnp.maximum(i - count // 2, 0))),
                whole(cotangent),
                pl.BlockSpec((wide, features), lambda i, z: (group(i, z), 0)),
            ],
            out_specs=whole(sent),
            scratch_shapes=[pltpu.VMEM(cotangent.shape, F32)],
        ),
        out_shape=sent,
        cost_estimate=FREE,
    )(z.reshape(1), early, late, cotangent, weight)


def products_here(x, tokens, cotangent, weight):
    count = 4
    rows = cotangent.shape[0]
    wide = weight.shape[0] // count

    def body(_, tokens_ref, cotangent_ref, weight_ref, keys_ref, grads_ref):
        @pl.when(pl.program_id(0) == 0)
        def _():
            keys_ref[...] = jnp.zeros_like(keys_ref)

        keys_ref[...] += dot(tokens_ref[...], weight_ref[...])
        grads_ref[...] = dot_t(cotangent_ref[...], weight_ref[...]).astype(BF16)

    here = pl.BlockSpec((rows, wide), lambda i, x: (0, x[0] * count + i))
    return pl.pallas_call(
        body,
        grid_spec=pltpu.PrefetchScalarGridSpec(
            num_scalar_prefetch=1,
            grid=(count,),
            in_specs=[
                here,
                whole(cotangent),
                pl.BlockSpec((wide, weight.shape[1]), lambda i, x: (i, 0)),
            ],
            out_specs=[whole(cotangent), here],
        ),
        out_shape=[
            jax.ShapeDtypeStruct(cotangent.shape, F32),
            jax.ShapeDtypeStruct(tokens.shape, BF16),
        ],
        cost_estimate=FREE,
    )(x.reshape(1), tokens, cotangent, weight)


def finish(x, keys, grads, back):
    count = 5
    rows, features = keys.shape
    wide = grads.shape[1] // (2 * count)

    def body(_, __, keys_ref, coded_ref, back_ref, out_ref, grads_ref):
        @pl.when(pl.program_id(0) == 0)
        def _():
            power = coded_ref[:rows, :].astype(F32)
            size = jnp.exp2(jnp.log2(jnp.abs(power)) * (1.0 / 16.0))
            size = jnp.where(power == 0, 0.0, size) * (coded_ref[rows:, :].astype(F32)[:1] / TOP)
            out_ref[...] = (keys_ref[...] + jnp.where(power < 0, -size, size)).astype(BF16)

        grads_ref[...] = back_ref[...]

    return pl.pallas_call(
        body,
        grid_spec=pltpu.PrefetchScalarGridSpec(
            num_scalar_prefetch=1,
            grid=(count,),
            in_specs=[
                pl.BlockSpec(memory_space=pl.ANY),
                whole(keys),
                pl.BlockSpec((rows + 16, features), lambda i, x: (0, 0)),
                pl.BlockSpec((rows, wide), lambda i, x: (0, features // wide + i)),
            ],
            out_specs=[
                whole(keys),
                pl.BlockSpec((rows, wide), lambda i, x: (0, (1 - x[0]) * count + i)),
            ],
        ),
        out_shape=[
            jax.ShapeDtypeStruct(keys.shape, BF16),
            jax.ShapeDtypeStruct(grads.shape, BF16),
        ],
        input_output_aliases={1: 1},
        cost_estimate=FREE,
    )(x.reshape(1), grads, keys, back, back)


def shards(activations, key_weights, key_cotangent, fragment, pseudo_grads, momentum):
    tokens, weight, cotangent, pseudo = (
        a[0] for a in (activations, key_weights, key_cotangent, pseudo_grads)
    )
    y, xh, c, x, z = (lax.axis_index(a) for a in SIZES)
    order = Sequence()
    half = tokens.shape[1] // 2
    rows = pseudo.shape[0] // 2
    mine, theirs = c * rows, (1 - c) * rows
    width = momentum.shape[1]
    pair = 2 * width
    quarter = 2 * pair
    chunk = half // N_Z
    odd_z = z % 2
    sign = 1 - 2 * odd_z
    group = z // 2
    early = [(group + 2) % 4, (group + 4 + sign) % 4]
    late = [group, (group + 4 - sign) % 4]

    def token_columns(array, side, groups):
        parts = [columns_of(array, side * half + g * 2 * chunk, 2 * chunk) for g in groups]
        return jnp.concatenate(parts, axis=1)

    weight_half = lax.all_gather(weight, "z", axis=0, tiled=True)
    cotangent_other = swap(cotangent, "xl")

    give = rows_of(pseudo, theirs, rows)
    order.did(give)
    pseudo_other = swap(give, "c")
    peaks = local_peaks(order.step(tokens), cotangent)
    order.did(peaks)
    peaks_other = swap(peaks, "xl")
    sent = token_columns(order.step(tokens), 1 - x, early)
    order.did(sent)
    early_other = swap(sent, "xl")
    pseudo_other = order.step(pseudo_other)
    total = rows_of(pseudo, mine, rows) + pseudo_other
    gives = [columns_of(total, (y ^ m) * quarter, quarter) for m in (1, 2, 3)]
    old_give = rows_of(momentum, theirs, rows)
    order.did(*gives, old_give)
    others = [swap(g, "y", m) for g, m in zip(gives, (1, 2, 3))]
    old_other = swap(old_give, "c")
    tokens_held, cotangent_other = order.step(tokens, cotangent_other)
    sent = token_columns(tokens_held, 1 - x, late)
    order.did(sent)
    late_other = swap(sent, "xl")
    peaks = join_peaks(peaks, order.step(peaks_other))
    order.did(peaks)
    peaks_other = swap(peaks, "z", 1)
    early_mine = token_columns(order.step(tokens), x, early)
    order.did(early_mine)
    peaks = join_peaks(peaks, order.step(peaks_other))
    order.did(peaks)
    peaks_other = swap(peaks, "z", 2)
    *others, old_other = order.step(*others, old_other)
    summed = columns_of(total, y * quarter, quarter) + others[0] + others[1] + others[2]
    give = columns_of(summed, (1 - xh) * pair, pair)
    order.did(summed, give)
    summed_other = swap(give, "xh")
    peaks = join_peaks(peaks, order.step(peaks_other))
    order.did(peaks)
    peaks_other = swap(peaks, "z", 4)

    def product(first, second):
        return lax.dot_general(
            jnp.concatenate([first, second], axis=0),
            jnp.concatenate([cotangent, cotangent_other], axis=0),
            (((0,), (0,)), ((), ())),
            preferred_element_type=F32,
        )

    early_other = order.step(early_other)
    partial_early = product(early_mine, early_other)
    order.did(partial_early)
    peaks = join_peaks(peaks, order.step(peaks_other))
    bound = jnp.maximum(peaks[0, 0] * peaks[4, 0], 1e-32)
    scale, back = 240.0 / bound, bound / (64.0 * 240.0)
    place = {4: odd_z, -3: 1 - odd_z, 2: 2 + odd_z, 3: 3 - odd_z}
    place_late = {0: odd_z, 1: 1 - odd_z, -2: 2 + odd_z, -1: 3 - odd_z}

    def own(distance, start=0, size=chunk):
        if distance in place:
            return rows_of(partial_early, place[distance] * chunk + start, size) * scale
        return rows_of(partial_late, place_late[distance] * chunk + start, size) * scale

    def send(value, pairs):
        message = encode(value)
        order.did(message)
        return lax.ppermute(message, "z", pairs)

    def ring_step(distance, even_in, odd_in):
        odd_out = send(own(-distance) + decode(order.step(even_in)), ODD)
        even_out = send(own(distance) + decode(order.step(odd_in)), EVEN)
        return even_out, odd_out

    part = chunk // 2
    far_even = send(own(4, 0, part), EVEN)
    far_odd = send(own(4, part, part), ODD)

    late_other = order.step(late_other)
    late_mine = token_columns(tokens, x, late)
    partial_late = product(late_mine, late_other)
    order.did(partial_late)

    summed_other = order.step(summed_other)
    average = (columns_of(summed, xh * pair, pair) + summed_other) / 16
    old = in_order(c, rows_of(momentum, mine, rows), old_other, 1)
    new = NESTEROV * old + average
    here = lax.dynamic_slice(fragment, (mine, (2 * y + xh) * pair), (rows, pair))
    updated = (here.astype(F32) - OUTER_RATE * (average + NESTEROV * new)).astype(BF16)
    keep = jnp.where(c == 0, new[:, :width], new[:, width:])
    give = jnp.where(c == 0, new[:, width:], new[:, :width])
    order.did(updated, keep, give)
    updated_other = swap(updated, "xh")
    new_other = swap(give, "c")

    updated_other = order.step(updated_other)
    wide = assemble(xh, lambda i: (i, 1 - i), (updated, updated_other), 1)
    order.did(wide)
    wides = [swap(wide, "y", m) for m in (1, 2, 3)]

    far_even, far_odd = order.step(far_even, far_odd)
    odd = jnp.concatenate([own(-3, 0, part) + decode(far_even), own(-3, part, part)])
    odd = send(odd, ODD)
    even = jnp.concatenate([own(3, 0, part), own(3, part, part) + decode(far_odd)])
    even = send(even, EVEN)

    wides = order.step(*wides)
    block = assemble(y, lambda i: (i, i ^ 1, i ^ 2, i ^ 3), (wide, *wides), 1)
    order.did(block)
    block_other = swap(block, "c")

    weight_half = order.step(weight_half)
    sent = products_for_partner(z, early_other, late_other, cotangent_other, weight_half)
    order.did(sent)
    products_back = swap(sent, "xl")

    even, odd = ring_step(2, even, odd)

    keys_mine, grads_mine = products_here(order.step(x), tokens, cotangent, weight_half)
    order.did(keys_mine, grads_mine)
    new_momentum = assemble(c, lambda i: (i, 1 - i), (keep, order.step(new_other)), 0)
    order.did(new_momentum)
    new_fragment = assemble(c, lambda i: (i, 1 - i), (block, order.step(block_other)), 0)
    order.did(new_fragment)

    even, odd = order.step(even, odd)
    even, odd = encode(own(1) + decode(odd)), encode(own(-1) + decode(even))
    order.did(even, odd)
    even, odd = lax.ppermute(even, "z", EVEN), lax.ppermute(odd, "z", ODD)

    products_back = order.step(products_back)
    key_out, act_grad = finish(x, keys_mine, grads_mine, products_back)
    order.did(key_out, act_grad)
    even, odd = order.step(even, odd)
    weight_grad = ((own(0) + decode(even) + decode(odd)) * back).astype(BF16)
    order.did(weight_grad)
    return (
        key_out[None],
        act_grad[None],
        weight_grad[None],
        new_fragment,
        new_momentum,
    )


def solution(mesh):
    fine = Mesh(mesh.devices.reshape(tuple(SIZES.values())), tuple(SIZES))
    return jax.shard_map(
        shards,
        mesh=fine,
        in_specs=(
            P(REP, FSDP, None),
            P(REP, FSDP, None),
            P(REP, FSDP, None),
            P(FSDP, None),
            P(REP, FSDP, None),
            P(FSDP, REP),
        ),
        out_specs=(
            P(REP, FSDP, None),
            P(REP, FSDP, None),
            P(REP, FSDP, None),
            P(FSDP, None),
            P(FSDP, REP),
        ),
        check_vma=False,
    )
```

```python
import jax
import jax.numpy as jnp
from jax import lax
from jax.experimental import pallas as pl
from jax.experimental.pallas import tpu as pltpu
from jax.sharding import Mesh
from jax.sharding import PartitionSpec as P

OUTER_RATE = 0.7
NESTEROV = 0.9
BF16 = jnp.bfloat16
F32 = jnp.float32
F16 = jnp.float16

SIZES = {"y": 4, "xh": 2, "c": 2, "xl": 2, "z": 8}
REP = ("y", "xh", "c")
FSDP = ("xl", "z")
N_Z = 8
EVEN = [(i, i ^ 1) for i in range(N_Z)]
ODD = [(i, (i - 1) % N_Z if i % 2 == 0 else (i + 1) % N_Z) for i in range(N_Z)]


def swap(value, axis, mask=1):
    return lax.ppermute(value, axis, [(i, i ^ mask) for i in range(SIZES[axis])])


class Sequence:
    def __init__(self):
        self.last = ()

    def step(self, *values):
        held = lax.optimization_barrier((*values, *self.last))[: len(values)]
        return held[0] if len(held) == 1 else held

    def did(self, *values):
        self.last = values


def rows_of(array, start, size):
    return lax.dynamic_slice_in_dim(array, start, size, 0)


def columns_of(array, start, size):
    return lax.dynamic_slice_in_dim(array, start, size, 1)


def in_order(here, mine, theirs, axis):
    first = here == 0
    return jnp.concatenate(
        [jnp.where(first, mine, theirs), jnp.where(first, theirs, mine)], axis=axis
    )


def encode(scaled):
    return (scaled * jnp.abs(scaled)).astype(F16)


def decode(sent):
    wide = sent.astype(F32)
    return jnp.sign(wide) * jnp.sqrt(jnp.abs(wide))


def tile_rows():
    return lax.broadcasted_iota(jnp.int32, (8, 128), 0)


def local_peaks(tokens, cotangent):
    peak = jnp.max(jnp.sum(jnp.abs(tokens.astype(F32)), axis=0))
    return jnp.where(tile_rows() < 4, peak, jnp.max(jnp.abs(cotangent)).astype(F32))


def join_peaks(peaks, other):
    return jnp.where(tile_rows() < 4, peaks + other, jnp.maximum(peaks, other))


def dot(left, right):
    return jnp.dot(left, right, preferred_element_type=F32)


def dot_t(left, right):
    return lax.dot_general(left, right, (((1,), (1,)), ((), ())), preferred_element_type=F32)


FREE = pl.CostEstimate(flops=0, bytes_accessed=0, transcendentals=0)


def whole(array):
    return pl.BlockSpec(array.shape, lambda i, *_: (0, 0))


def assemble(here, places, pieces, axis):
    size = pieces[0].shape[axis]

    def body(here_ref, *refs):
        out_ref = refs[-1]
        for place, piece_ref in zip(places(here_ref[0]), refs[:-1]):
            at = pl.ds(pl.multiple_of(place * size, 32 if axis == 0 else 128), size)
            if axis == 0:
                out_ref[at, :] = piece_ref[...]
            else:
                out_ref[:, at] = piece_ref[...]

    shape = list(pieces[0].shape)
    shape[axis] *= len(pieces)
    out = jax.ShapeDtypeStruct(tuple(shape), pieces[0].dtype)
    return pl.pallas_call(
        body,
        grid_spec=pltpu.PrefetchScalarGridSpec(
            num_scalar_prefetch=1,
            grid=(1,),
            in_specs=[whole(p) for p in pieces],
            out_specs=whole(out),
        ),
        out_shape=out,
        cost_estimate=FREE,
    )(here.reshape(1), *pieces)


TOP = 220.0


def products_for_partner(z, early, late, cotangent, weight):
    count = 4
    rows, features = cotangent.shape
    wide = weight.shape[0] // count

    def group(i, z_ref):
        step = 1 - 2 * (z_ref[0] % 2)
        return (z_ref[0] // 2 + jnp.where(i % 2 == 1, 4 + step * (2 - i), 2 - i)) % 4

    def body(z_ref, early_ref, late_ref, cotangent_ref, weight_ref, sent_ref, keys_ref):
        i = pl.program_id(0)

        @pl.when(i == 0)
        def _():
            keys_ref[...] = jnp.zeros_like(keys_ref)

        tokens = jnp.where(i < count // 2, early_ref[...], late_ref[...])
        keys_ref[...] += dot(tokens, weight_ref[...])
        place = pl.multiple_of(features + group(i, z_ref) * wide, 128)
        grads = dot_t(cotangent_ref[...], weight_ref[...]).astype(BF16)
        sent_ref[:rows, pl.ds(place, wide)] = grads

        @pl.when(i == count - 1)
        def _():
            keys = keys_ref[...]
            largest = jnp.maximum(jnp.max(jnp.abs(keys)) * 1.01, 1e-30)
            sent = jnp.full((16, features), largest, F32).astype(BF16)
            sent_ref[rows:, :features] = sent
            sent_ref[rows:, features:] = jnp.zeros((16, weight.shape[0]), BF16)
            scaled = keys * (TOP / sent[:1, :].astype(F32))
            power = scaled * scaled
            power = power * power
            power = power * power
            power = power * power
            sent_ref[:rows, :features] = jnp.where(scaled < 0, -power, power).astype(BF16)

    sent = jax.ShapeDtypeStruct((rows + 16, features + weight.shape[0]), BF16)
    return pl.pallas_call(
        body,
        grid_spec=pltpu.PrefetchScalarGridSpec(
            num_scalar_prefetch=1,
            grid=(count,),
            in_specs=[
                pl.BlockSpec((rows, wide), lambda i, z: (0, jnp.minimum(i, count // 2 - 1))),
                pl.BlockSpec((rows, wide), lambda i, z: (0, jnp.maximum(i - count // 2, 0))),
                whole(cotangent),
                pl.BlockSpec((wide, features), lambda i, z: (group(i, z), 0)),
            ],
            out_specs=whole(sent),
            scratch_shapes=[pltpu.VMEM(cotangent.shape, F32)],
        ),
        out_shape=sent,
        cost_estimate=FREE,
    )(z.reshape(1), early, late, cotangent, weight)


def products_here(x, tokens, cotangent, weight):
    count = 4
    rows = cotangent.shape[0]
    wide = weight.shape[0] // count

    def body(_, tokens_ref, cotangent_ref, weight_ref, keys_ref, grads_ref):
        @pl.when(pl.program_id(0) == 0)
        def _():
            keys_ref[...] = jnp.zeros_like(keys_ref)

        keys_ref[...] += dot(tokens_ref[...], weight_ref[...])
        grads_ref[...] = dot_t(cotangent_ref[...], weight_ref[...]).astype(BF16)

    here = pl.BlockSpec((rows, wide), lambda i, x: (0, x[0] * count + i))
    return pl.pallas_call(
        body,
        grid_spec=pltpu.PrefetchScalarGridSpec(
            num_scalar_prefetch=1,
            grid=(count,),
            in_specs=[
                here,
                whole(cotangent),
                pl.BlockSpec((wide, weight.shape[1]), lambda i, x: (i, 0)),
            ],
            out_specs=[whole(cotangent), here],
        ),
        out_shape=[
            jax.ShapeDtypeStruct(cotangent.shape, F32),
            jax.ShapeDtypeStruct(tokens.shape, BF16),
        ],
        cost_estimate=FREE,
    )(x.reshape(1), tokens, cotangent, weight)


def finish(x, keys, grads, back):
    count = 5
    rows, features = keys.shape
    wide = grads.shape[1] // (2 * count)

    def body(_, __, keys_ref, coded_ref, back_ref, out_ref, grads_ref):
        @pl.when(pl.program_id(0) == 0)
        def _():
            power = coded_ref[:rows, :].astype(F32)
            size = jnp.exp2(jnp.log2(jnp.abs(power)) * (1.0 / 16.0))
            size = jnp.where(power == 0, 0.0, size) * (coded_ref[rows:, :].astype(F32)[:1] / TOP)
            out_ref[...] = (keys_ref[...] + jnp.where(power < 0, -size, size)).astype(BF16)

        grads_ref[...] = back_ref[...]

    return pl.pallas_call(
        body,
        grid_spec=pltpu.PrefetchScalarGridSpec(
            num_scalar_prefetch=1,
            grid=(count,),
            in_specs=[
                pl.BlockSpec(memory_space=pl.ANY),
                whole(keys),
                pl.BlockSpec((rows + 16, features), lambda i, x: (0, 0)),
                pl.BlockSpec((rows, wide), lambda i, x: (0, features // wide + i)),
            ],
            out_specs=[
                whole(keys),
                pl.BlockSpec((rows, wide), lambda i, x: (0, (1 - x[0]) * count + i)),
            ],
        ),
        out_shape=[
            jax.ShapeDtypeStruct(keys.shape, BF16),
            jax.ShapeDtypeStruct(grads.shape, BF16),
        ],
        input_output_aliases={1: 1},
        cost_estimate=FREE,
    )(x.reshape(1), grads, keys, back, back)


def shards(activations, key_weights, key_cotangent, fragment, pseudo_grads, momentum):
    tokens, weight, cotangent, pseudo = (
        a[0] for a in (activations, key_weights, key_cotangent, pseudo_grads)
    )
    y, xh, c, x, z = (lax.axis_index(a) for a in SIZES)
    order = Sequence()
    half = tokens.shape[1] // 2
    rows = pseudo.shape[0] // 2
    mine, theirs = c * rows, (1 - c) * rows
    width = momentum.shape[1]
    pair = 2 * width
    quarter = 2 * pair
    chunk = half // N_Z
    odd_z = z % 2
    sign = 1 - 2 * odd_z
    group = z // 2
    early = [(group + 2) % 4, (group + 4 + sign) % 4]
    late = [group, (group + 4 - sign) % 4]

    def token_columns(array, side, groups):
        parts = [columns_of(array, side * half + g * 2 * chunk, 2 * chunk) for g in groups]
        return jnp.concatenate(parts, axis=1)

    weight_half = lax.all_gather(weight, "z", axis=0, tiled=True)
    cotangent_other = swap(cotangent, "xl")

    give = rows_of(pseudo, theirs, rows)
    order.did(give)
    pseudo_other = swap(give, "c")
    peaks = local_peaks(order.step(tokens), cotangent)
    order.did(peaks)
    peaks_other = swap(peaks, "xl")
    sent = token_columns(order.step(tokens), 1 - x, early)
    order.did(sent)
    early_other = swap(sent, "xl")
    pseudo_other = order.step(pseudo_other)
    total = rows_of(pseudo, mine, rows) + pseudo_other
    gives = [columns_of(total, (y ^ m) * quarter, quarter) for m in (1, 2, 3)]
    old_give = rows_of(momentum, theirs, rows)
    order.did(*gives, old_give)
    others = [swap(g, "y", m) for g, m in zip(gives, (1, 2, 3))]
    old_other = swap(old_give, "c")
    sent = token_columns(order.step(tokens), 1 - x, late)
    order.did(sent)
    late_other = swap(sent, "xl")
    peaks = join_peaks(peaks, order.step(peaks_other))
    order.did(peaks)
    peaks_other = swap(peaks, "z", 1)
    early_mine = token_columns(order.step(tokens), x, early)
    order.did(early_mine)
    peaks = join_peaks(peaks, order.step(peaks_other))
    order.did(peaks)
    peaks_other = swap(peaks, "z", 2)
    *others, old_other = order.step(*others, old_other)
    summed = columns_of(total, y * quarter, quarter) + others[0] + others[1] + others[2]
    give = columns_of(summed, (1 - xh) * pair, pair)
    order.did(summed, give)
    summed_other = swap(give, "xh")
    peaks = join_peaks(peaks, order.step(peaks_other))
    order.did(peaks)
    peaks_other = swap(peaks, "z", 4)

    def product(first, second):
        return lax.dot_general(
            jnp.concatenate([first, second], axis=0),
            jnp.concatenate([cotangent, cotangent_other], axis=0),
            (((0,), (0,)), ((), ())),
            preferred_element_type=F32,
        )

    early_other, cotangent_other = order.step(early_other, cotangent_other)
    partial_early = product(early_mine, early_other)
    order.did(partial_early)
    peaks = join_peaks(peaks, order.step(peaks_other))
    bound = jnp.maximum(peaks[0, 0] * peaks[4, 0], 1e-32)
    scale, back = 240.0 / bound, bound / (64.0 * 240.0)
    place = {4: odd_z, -3: 1 - odd_z, 2: 2 + odd_z, 3: 3 - odd_z}
    place_late = {0: odd_z, 1: 1 - odd_z, -2: 2 + odd_z, -1: 3 - odd_z}

    def own(distance, start=0, size=chunk):
        if distance in place:
            return rows_of(partial_early, place[distance] * chunk + start, size) * scale
        return rows_of(partial_late, place_late[distance] * chunk + start, size) * scale

    def send(value, pairs):
        message = encode(value)
        order.did(message)
        return lax.ppermute(message, "z", pairs)

    def ring_step(distance, even_in, odd_in):
        odd_out = send(own(-distance) + decode(order.step(even_in)), ODD)
        even_out = send(own(distance) + decode(order.step(odd_in)), EVEN)
        return even_out, odd_out

    part = chunk // 2
    far_even = send(own(4, 0, part), EVEN)
    far_odd = send(own(4, part, part), ODD)

    late_other = order.step(late_other)
    late_mine = token_columns(tokens, x, late)
    partial_late = product(late_mine, late_other)
    order.did(partial_late)

    summed_other = order.step(summed_other)
    average = (columns_of(summed, xh * pair, pair) + summed_other) / 16
    old = in_order(c, rows_of(momentum, mine, rows), old_other, 1)
    new = NESTEROV * old + average
    here = lax.dynamic_slice(fragment, (mine, (2 * y + xh) * pair), (rows, pair))
    updated = (here.astype(F32) - OUTER_RATE * (average + NESTEROV * new)).astype(BF16)
    keep = jnp.where(c == 0, new[:, :width], new[:, width:])
    give = jnp.where(c == 0, new[:, width:], new[:, :width])
    order.did(updated, keep, give)
    updated_other = swap(updated, "xh")
    new_other = swap(give, "c")

    updated_other = order.step(updated_other)
    wide = assemble(xh, lambda i: (i, 1 - i), (updated, updated_other), 1)
    order.did(wide)
    wides = [swap(wide, "y", m) for m in (1, 2, 3)]

    far_even, far_odd = order.step(far_even, far_odd)
    odd = jnp.concatenate([own(-3, 0, part) + decode(far_even), own(-3, part, part)])
    odd = send(odd, ODD)
    even = jnp.concatenate([own(3, 0, part), own(3, part, part) + decode(far_odd)])
    even = send(even, EVEN)

    wides = order.step(*wides)
    block = assemble(y, lambda i: (i, i ^ 1, i ^ 2, i ^ 3), (wide, *wides), 1)
    order.did(block)
    block_other = swap(block, "c")

    weight_half = order.step(weight_half)
    sent = products_for_partner(z, early_other, late_other, cotangent_other, weight_half)
    order.did(sent)
    products_back = swap(sent, "xl")

    even, odd = ring_step(2, even, odd)

    keys_mine, grads_mine = products_here(order.step(x), tokens, cotangent, weight_half)
    order.did(keys_mine, grads_mine)
    new_momentum = assemble(c, lambda i: (i, 1 - i), (keep, order.step(new_other)), 0)
    order.did(new_momentum)
    new_fragment = assemble(c, lambda i: (i, 1 - i), (block, order.step(block_other)), 0)
    order.did(new_fragment)

    even, odd = order.step(even, odd)
    even, odd = encode(own(1) + decode(odd)), encode(own(-1) + decode(even))
    order.did(even, odd)
    even, odd = lax.ppermute(even, "z", EVEN), lax.ppermute(odd, "z", ODD)

    products_back = order.step(products_back)
    key_out, act_grad = finish(x, keys_mine, grads_mine, products_back)
    order.did(key_out, act_grad)
    even, odd = order.step(even, odd)
    weight_grad = ((own(0) + decode(even) + decode(odd)) * back).astype(BF16)
    order.did(weight_grad)
    return (
        key_out[None],
        act_grad[None],
        weight_grad[None],
        new_fragment,
        new_momentum,
    )


def solution(mesh):
    fine = Mesh(mesh.devices.reshape(tuple(SIZES.values())), tuple(SIZES))
    return jax.shard_map(
        shards,
        mesh=fine,
        in_specs=(
            P(REP, FSDP, None),
            P(REP, FSDP, None),
            P(REP, FSDP, None),
            P(FSDP, None),
            P(REP, FSDP, None),
            P(FSDP, REP),
        ),
        out_specs=(
            P(REP, FSDP, None),
            P(REP, FSDP, None),
            P(REP, FSDP, None),
            P(FSDP, None),
            P(FSDP, REP),
        ),
        check_vma=False,
    )
```

```python
import jax
import jax.numpy as jnp
from jax import lax
from jax.experimental import pallas as pl
from jax.experimental.pallas import tpu as pltpu
from jax.sharding import Mesh
from jax.sharding import PartitionSpec as P

OUTER_RATE = 0.7
NESTEROV = 0.9
BF16 = jnp.bfloat16
F32 = jnp.float32
F16 = jnp.float16

SIZES = {"y": 4, "xh": 2, "c": 2, "xl": 2, "z": 8}
REP = ("y", "xh", "c")
FSDP = ("xl", "z")
N_Z = 8
EVEN = [(i, i ^ 1) for i in range(N_Z)]
ODD = [(i, (i - 1) % N_Z if i % 2 == 0 else (i + 1) % N_Z) for i in range(N_Z)]


def swap(value, axis, mask=1):
    return lax.ppermute(value, axis, [(i, i ^ mask) for i in range(SIZES[axis])])


class Sequence:
    def __init__(self):
        self.last = ()

    def step(self, *values):
        held = lax.optimization_barrier((*values, *self.last))[: len(values)]
        return held[0] if len(held) == 1 else held

    def did(self, *values):
        self.last = values


def rows_of(array, start, size):
    return lax.dynamic_slice_in_dim(array, start, size, 0)


def columns_of(array, start, size):
    return lax.dynamic_slice_in_dim(array, start, size, 1)


def in_order(here, mine, theirs, axis):
    first = here == 0
    return jnp.concatenate(
        [jnp.where(first, mine, theirs), jnp.where(first, theirs, mine)], axis=axis
    )


def encode(scaled):
    return (scaled * jnp.abs(scaled)).astype(F16)


def decode(sent):
    wide = sent.astype(F32)
    return jnp.sign(wide) * jnp.sqrt(jnp.abs(wide))


def tile_rows():
    return lax.broadcasted_iota(jnp.int32, (8, 128), 0)


def local_peaks(tokens, cotangent):
    peak = jnp.max(jnp.sum(jnp.abs(tokens.astype(F32)), axis=0))
    return jnp.where(tile_rows() < 4, peak, jnp.max(jnp.abs(cotangent)).astype(F32))


def join_peaks(peaks, other):
    return jnp.where(tile_rows() < 4, peaks + other, jnp.maximum(peaks, other))


def dot(left, right):
    return jnp.dot(left, right, preferred_element_type=F32)


def dot_t(left, right):
    return lax.dot_general(left, right, (((1,), (1,)), ((), ())), preferred_element_type=F32)


FREE = pl.CostEstimate(flops=0, bytes_accessed=0, transcendentals=0)


def whole(array):
    return pl.BlockSpec(array.shape, lambda i, *_: (0, 0))


def assemble(here, places, pieces, axis):
    size = pieces[0].shape[axis]

    def body(here_ref, *refs):
        out_ref = refs[-1]
        for place, piece_ref in zip(places(here_ref[0]), refs[:-1]):
            at = pl.ds(pl.multiple_of(place * size, 32 if axis == 0 else 128), size)
            if axis == 0:
                out_ref[at, :] = piece_ref[...]
            else:
                out_ref[:, at] = piece_ref[...]

    shape = list(pieces[0].shape)
    shape[axis] *= len(pieces)
    out = jax.ShapeDtypeStruct(tuple(shape), pieces[0].dtype)
    return pl.pallas_call(
        body,
        grid_spec=pltpu.PrefetchScalarGridSpec(
            num_scalar_prefetch=1,
            grid=(1,),
            in_specs=[whole(p) for p in pieces],
            out_specs=whole(out),
        ),
        out_shape=out,
        cost_estimate=FREE,
    )(here.reshape(1), *pieces)


TOP = 220.0


def lay_chunks(z, chunks, halves):
    size = chunks[0][0].shape[0]
    count = N_Z
    pieces = [(c, d, 0) for c, d in chunks]
    pieces += [(h, 4, k * (size // 2)) for k, h in enumerate(halves)]

    def body(z_ref, *refs):
        *piece_refs, out_ref, sems = refs
        here = z_ref[0]
        sign = 1 - 2 * (here % 2)
        copies = []
        for k, (ref, (piece, distance, offset)) in enumerate(zip(piece_refs, pieces)):
            start = (here + count + distance * sign) % count * size + offset
            at = pl.ds(pl.multiple_of(start, 32), piece.shape[0])
            copies.append(pltpu.make_async_copy(ref, out_ref.at[at, :], sems.at[k]))
        for copy in copies:
            copy.start()
        for copy in copies:
            copy.wait()

    hbm = pl.BlockSpec(memory_space=pl.ANY)
    first = chunks[0][0]
    return pl.pallas_call(
        body,
        grid_spec=pltpu.PrefetchScalarGridSpec(
            num_scalar_prefetch=1,
            grid=(1,),
            in_specs=[hbm] * len(pieces),
            out_specs=hbm,
            scratch_shapes=[pltpu.SemaphoreType.DMA((len(pieces),))],
        ),
        out_shape=jax.ShapeDtypeStruct((count * size, first.shape[1]), first.dtype),
        cost_estimate=FREE,
    )(z.reshape(1), *(p for p, _, _ in pieces))


def products_for_partner(z, early, late, cotangent, weight):
    count = 4
    rows, features = cotangent.shape
    wide = weight.shape[0] // count

    def group(i, z_ref):
        step = 1 - 2 * (z_ref[0] % 2)
        return (z_ref[0] // 2 + jnp.where(i % 2 == 1, 4 + step * (2 - i), 2 - i)) % 4

    def body(z_ref, early_ref, late_ref, cotangent_ref, weight_ref, sent_ref, keys_ref):
        i = pl.program_id(0)

        @pl.when(i == 0)
        def _():
            keys_ref[...] = jnp.zeros_like(keys_ref)

        tokens = jnp.where(i < count // 2, early_ref[...], late_ref[...])
        keys_ref[...] += dot(tokens, weight_ref[...])
        place = pl.multiple_of(features + group(i, z_ref) * wide, 128)
        grads = dot_t(cotangent_ref[...], weight_ref[...]).astype(BF16)
        sent_ref[:rows, pl.ds(place, wide)] = grads

        @pl.when(i == count - 1)
        def _():
            keys = keys_ref[...]
            largest = jnp.maximum(jnp.max(jnp.abs(keys)) * 1.01, 1e-30)
            sent = jnp.full((16, features), largest, F32).astype(BF16)
            sent_ref[rows:, :features] = sent
            sent_ref[rows:, features:] = jnp.zeros((16, weight.shape[0]), BF16)
            scaled = keys * (TOP / sent[:1, :].astype(F32))
            power = scaled * scaled
            power = power * power
            power = power * power
            power = power * power
            sent_ref[:rows, :features] = jnp.where(scaled < 0, -power, power).astype(BF16)

    sent = jax.ShapeDtypeStruct((rows + 16, features + weight.shape[0]), BF16)
    return pl.pallas_call(
        body,
        grid_spec=pltpu.PrefetchScalarGridSpec(
            num_scalar_prefetch=1,
            grid=(count,),
            in_specs=[
                pl.BlockSpec((rows, wide), lambda i, z: (0, jnp.minimum(i, count // 2 - 1))),
                pl.BlockSpec((rows, wide), lambda i, z: (0, jnp.maximum(i - count // 2, 0))),
                whole(cotangent),
                pl.BlockSpec((wide, features), lambda i, z: (group(i, z), 0)),
            ],
            out_specs=whole(sent),
            scratch_shapes=[pltpu.VMEM(cotangent.shape, F32)],
        ),
        out_shape=sent,
        cost_estimate=FREE,
    )(z.reshape(1), early, late, cotangent, weight)


def products_here(x, tokens, cotangent, weight):
    count = 4
    rows = cotangent.shape[0]
    wide = weight.shape[0] // count

    def body(_, tokens_ref, cotangent_ref, weight_ref, keys_ref, grads_ref):
        @pl.when(pl.program_id(0) == 0)
        def _():
            keys_ref[...] = jnp.zeros_like(keys_ref)

        keys_ref[...] += dot(tokens_ref[...], weight_ref[...])
        grads_ref[...] = dot_t(cotangent_ref[...], weight_ref[...]).astype(BF16)

    here = pl.BlockSpec((rows, wide), lambda i, x: (0, x[0] * count + i))
    return pl.pallas_call(
        body,
        grid_spec=pltpu.PrefetchScalarGridSpec(
            num_scalar_prefetch=1,
            grid=(count,),
            in_specs=[
                here,
                whole(cotangent),
                pl.BlockSpec((wide, weight.shape[1]), lambda i, x: (i, 0)),
            ],
            out_specs=[whole(cotangent), here],
        ),
        out_shape=[
            jax.ShapeDtypeStruct(cotangent.shape, F32),
            jax.ShapeDtypeStruct(tokens.shape, BF16),
        ],
        cost_estimate=FREE,
    )(x.reshape(1), tokens, cotangent, weight)


def finish(x, keys, grads, back):
    count = 5
    rows, features = keys.shape
    wide = grads.shape[1] // (2 * count)

    def body(_, __, keys_ref, coded_ref, back_ref, out_ref, grads_ref):
        @pl.when(pl.program_id(0) == 0)
        def _():
            power = coded_ref[:rows, :].astype(F32)
            size = jnp.exp2(jnp.log2(jnp.abs(power)) * (1.0 / 16.0))
            size = jnp.where(power == 0, 0.0, size) * (coded_ref[rows:, :].astype(F32)[:1] / TOP)
            out_ref[...] = (keys_ref[...] + jnp.where(power < 0, -size, size)).astype(BF16)

        grads_ref[...] = back_ref[...]

    return pl.pallas_call(
        body,
        grid_spec=pltpu.PrefetchScalarGridSpec(
            num_scalar_prefetch=1,
            grid=(count,),
            in_specs=[
                pl.BlockSpec(memory_space=pl.ANY),
                whole(keys),
                pl.BlockSpec((rows + 16, features), lambda i, x: (0, 0)),
                pl.BlockSpec((rows, wide), lambda i, x: (0, features // wide + i)),
            ],
            out_specs=[
                whole(keys),
                pl.BlockSpec((rows, wide), lambda i, x: (0, (1 - x[0]) * count + i)),
            ],
        ),
        out_shape=[
            jax.ShapeDtypeStruct(keys.shape, BF16),
            jax.ShapeDtypeStruct(grads.shape, BF16),
        ],
        input_output_aliases={1: 1},
        cost_estimate=FREE,
    )(x.reshape(1), grads, keys, back, back)


def shards(activations, key_weights, key_cotangent, fragment, pseudo_grads, momentum):
    tokens, weight, cotangent, pseudo = (
        a[0] for a in (activations, key_weights, key_cotangent, pseudo_grads)
    )
    y, xh, c, x, z = (lax.axis_index(a) for a in SIZES)
    order = Sequence()
    half = tokens.shape[1] // 2
    rows = pseudo.shape[0] // 2
    mine, theirs = c * rows, (1 - c) * rows
    width = momentum.shape[1]
    pair = 2 * width
    quarter = 2 * pair
    chunk = half // N_Z
    odd_z = z % 2
    sign = 1 - 2 * odd_z
    group = z // 2
    early = [(group + 2) % 4, (group + 4 + sign) % 4]
    late = [group, (group + 4 - sign) % 4]

    def token_columns(array, side, groups):
        parts = [columns_of(array, side * half + g * 2 * chunk, 2 * chunk) for g in groups]
        return jnp.concatenate(parts, axis=1)

    def pass_on(even, odd):
        return lax.ppermute(odd, "z", EVEN), lax.ppermute(even, "z", ODD)

    chunks = [(weight, 0)]
    weight_even, weight_odd = pass_on(weight, weight)

    def arrived(distance, even, odd):
        even, odd = order.step(even, odd)
        order.did(even, odd)
        chunks.extend([(even, distance), (odd, -distance)])
        return even, odd

    cotangent_other = swap(cotangent, "xl")

    give = rows_of(pseudo, theirs, rows)
    order.did(give)
    pseudo_other = swap(give, "c")
    peaks = local_peaks(order.step(tokens), cotangent)
    order.did(peaks)
    peaks_other = swap(peaks, "xl")
    sent = token_columns(order.step(tokens), 1 - x, early)
    order.did(sent)
    early_other = swap(sent, "xl")
    weight_even, weight_odd = pass_on(*arrived(1, weight_even, weight_odd))
    pseudo_other = order.step(pseudo_other)
    total = rows_of(pseudo, mine, rows) + pseudo_other
    gives = [columns_of(total, (y ^ m) * quarter, quarter) for m in (1, 2, 3)]
    old_give = rows_of(momentum, theirs, rows)
    order.did(*gives, old_give)
    others = [swap(g, "y", m) for g, m in zip(gives, (1, 2, 3))]
    old_other = swap(old_give, "c")
    sent = token_columns(order.step(tokens), 1 - x, late)
    order.did(sent)
    late_other = swap(sent, "xl")
    peaks = join_peaks(peaks, order.step(peaks_other))
    order.did(peaks)
    peaks_other = swap(peaks, "z", 1)
    early_mine = token_columns(order.step(tokens), x, early)
    order.did(early_mine)
    peaks = join_peaks(peaks, order.step(peaks_other))
    order.did(peaks)
    peaks_other = swap(peaks, "z", 2)
    weight_even, weight_odd = pass_on(*arrived(2, weight_even, weight_odd))
    *others, old_other = order.step(*others, old_other)
    summed = columns_of(total, y * quarter, quarter) + others[0] + others[1] + others[2]
    give = columns_of(summed, (1 - xh) * pair, pair)
    order.did(summed, give)
    summed_other = swap(give, "xh")
    peaks = join_peaks(peaks, order.step(peaks_other))
    order.did(peaks)
    peaks_other = swap(peaks, "z", 4)

    def product(first, second):
        return lax.dot_general(
            jnp.concatenate([first, second], axis=0),
            jnp.concatenate([cotangent, cotangent_other], axis=0),
            (((0,), (0,)), ((), ())),
            preferred_element_type=F32,
        )

    early_other, cotangent_other = order.step(early_other, cotangent_other)
    partial_early = product(early_mine, early_other)
    order.did(partial_early)
    weight_even, weight_odd = arrived(3, weight_even, weight_odd)
    top = weight.shape[0] // 2
    halves = pass_on(weight_even[top:], weight_odd[:top])
    peaks = join_peaks(peaks, order.step(peaks_other))
    bound = jnp.maximum(peaks[0, 0] * peaks[4, 0], 1e-32)
    scale, back = 240.0 / bound, bound / (64.0 * 240.0)
    place = {4: odd_z, -3: 1 - odd_z, 2: 2 + odd_z, 3: 3 - odd_z}
    place_late = {0: odd_z, 1: 1 - odd_z, -2: 2 + odd_z, -1: 3 - odd_z}

    def own(distance, start=0, size=chunk):
        if distance in place:
            return rows_of(partial_early, place[distance] * chunk + start, size) * scale
        return rows_of(partial_late, place_late[distance] * chunk + start, size) * scale

    def send(value, pairs):
        message = encode(value)
        order.did(message)
        return lax.ppermute(message, "z", pairs)

    def ring_step(distance, even_in, odd_in):
        odd_out = send(own(-distance) + decode(order.step(even_in)), ODD)
        even_out = send(own(distance) + decode(order.step(odd_in)), EVEN)
        return even_out, odd_out

    part = chunk // 2
    far_even = send(own(4, 0, part), EVEN)
    far_odd = send(own(4, part, part), ODD)

    late_other = order.step(late_other)
    late_mine = token_columns(tokens, x, late)
    partial_late = product(late_mine, late_other)
    order.did(partial_late)
    halves = order.step(*halves)
    order.did(*halves)

    summed_other = order.step(summed_other)
    average = (columns_of(summed, xh * pair, pair) + summed_other) / 16
    old = in_order(c, rows_of(momentum, mine, rows), old_other, 1)
    new = NESTEROV * old + average
    here = lax.dynamic_slice(fragment, (mine, (2 * y + xh) * pair), (rows, pair))
    updated = (here.astype(F32) - OUTER_RATE * (average + NESTEROV * new)).astype(BF16)
    keep = jnp.where(c == 0, new[:, :width], new[:, width:])
    give = jnp.where(c == 0, new[:, width:], new[:, :width])
    order.did(updated, keep, give)
    updated_other = swap(updated, "xh")
    new_other = swap(give, "c")

    far_even, far_odd = order.step(far_even, far_odd)
    odd = jnp.concatenate([own(-3, 0, part) + decode(far_even), own(-3, part, part)])
    odd = send(odd, ODD)
    even = jnp.concatenate([own(3, 0, part), own(3, part, part) + decode(far_odd)])
    even = send(even, EVEN)

    weight_half = lay_chunks(z, chunks, halves)
    order.did(weight_half)
    updated_other = order.step(updated_other)
    wide = assemble(xh, lambda i: (i, 1 - i), (updated, updated_other), 1)
    order.did(wide)
    wides = [swap(wide, "y", m) for m in (1, 2, 3)]

    early_held = order.step(early_other)
    sent = products_for_partner(z, early_held, late_other, cotangent_other, weight_half)
    order.did(sent)
    products_back = swap(sent, "xl")

    wides = order.step(*wides)
    block = assemble(y, lambda i: (i, i ^ 1, i ^ 2, i ^ 3), (wide, *wides), 1)
    order.did(block)
    block_other = swap(block, "c")

    even, odd = ring_step(2, even, odd)

    keys_mine, grads_mine = products_here(order.step(x), tokens, cotangent, weight_half)
    order.did(keys_mine, grads_mine)
    new_momentum = assemble(c, lambda i: (i, 1 - i), (keep, order.step(new_other)), 0)
    order.did(new_momentum)
    new_fragment = assemble(c, lambda i: (i, 1 - i), (block, order.step(block_other)), 0)
    order.did(new_fragment)

    even, odd = order.step(even, odd)
    even, odd = encode(own(1) + decode(odd)), encode(own(-1) + decode(even))
    order.did(even, odd)
    even, odd = lax.ppermute(even, "z", EVEN), lax.ppermute(odd, "z", ODD)

    products_back = order.step(products_back)
    key_out, act_grad = finish(x, keys_mine, grads_mine, products_back)
    order.did(key_out, act_grad)
    even, odd = order.step(even, odd)
    weight_grad = ((own(0) + decode(even) + decode(odd)) * back).astype(BF16)
    order.did(weight_grad)
    return (
        key_out[None],
        act_grad[None],
        weight_grad[None],
        new_fragment,
        new_momentum,
    )


def solution(mesh):
    fine = Mesh(mesh.devices.reshape(tuple(SIZES.values())), tuple(SIZES))
    return jax.shard_map(
        shards,
        mesh=fine,
        in_specs=(
            P(REP, FSDP, None),
            P(REP, FSDP, None),
            P(REP, FSDP, None),
            P(FSDP, None),
            P(REP, FSDP, None),
            P(FSDP, REP),
        ),
        out_specs=(
            P(REP, FSDP, None),
            P(REP, FSDP, None),
            P(REP, FSDP, None),
            P(FSDP, None),
            P(FSDP, REP),
        ),
        check_vma=False,
    )
```

```python
import jax
import jax.numpy as jnp
from jax import lax
from jax.experimental import pallas as pl
from jax.experimental.pallas import tpu as pltpu
from jax.sharding import Mesh
from jax.sharding import PartitionSpec as P

OUTER_RATE = 0.7
NESTEROV = 0.9
BF16 = jnp.bfloat16
F32 = jnp.float32
F16 = jnp.float16

SIZES = {"y": 4, "xh": 2, "c": 2, "xl": 2, "z": 8}
REP = ("y", "xh", "c")
FSDP = ("xl", "z")
N_Z = 8
EVEN = [(i, i ^ 1) for i in range(N_Z)]
ODD = [(i, (i - 1) % N_Z if i % 2 == 0 else (i + 1) % N_Z) for i in range(N_Z)]


def swap(value, axis, mask=1):
    return lax.ppermute(value, axis, [(i, i ^ mask) for i in range(SIZES[axis])])


class Sequence:
    def __init__(self):
        self.last = ()

    def step(self, *values):
        held = lax.optimization_barrier((*values, *self.last))[: len(values)]
        return held[0] if len(held) == 1 else held

    def did(self, *values):
        self.last = values


def rows_of(array, start, size):
    return lax.dynamic_slice_in_dim(array, start, size, 0)


def columns_of(array, start, size):
    return lax.dynamic_slice_in_dim(array, start, size, 1)


def in_order(here, mine, theirs, axis):
    first = here == 0
    return jnp.concatenate(
        [jnp.where(first, mine, theirs), jnp.where(first, theirs, mine)], axis=axis
    )


def encode(scaled):
    return (scaled * jnp.abs(scaled)).astype(F16)


def decode(sent):
    wide = sent.astype(F32)
    return jnp.sign(wide) * jnp.sqrt(jnp.abs(wide))


def tile_rows():
    return lax.broadcasted_iota(jnp.int32, (8, 128), 0)


def local_peaks(tokens, cotangent):
    peak = jnp.max(jnp.sum(jnp.abs(tokens.astype(F32)), axis=0))
    return jnp.where(tile_rows() < 4, peak, jnp.max(jnp.abs(cotangent)).astype(F32))


def join_peaks(peaks, other):
    return jnp.where(tile_rows() < 4, peaks + other, jnp.maximum(peaks, other))


def dot(left, right):
    return jnp.dot(left, right, preferred_element_type=F32)


def dot_t(left, right):
    return lax.dot_general(left, right, (((1,), (1,)), ((), ())), preferred_element_type=F32)


FREE = pl.CostEstimate(flops=0, bytes_accessed=0, transcendentals=0)


def whole(array):
    return pl.BlockSpec(array.shape, lambda i, *_: (0, 0))


def assemble(here, places, pieces, axis):
    size = pieces[0].shape[axis]

    def body(here_ref, *refs):
        out_ref = refs[-1]
        for place, piece_ref in zip(places(here_ref[0]), refs[:-1]):
            at = pl.ds(pl.multiple_of(place * size, 32 if axis == 0 else 128), size)
            if axis == 0:
                out_ref[at, :] = piece_ref[...]
            else:
                out_ref[:, at] = piece_ref[...]

    shape = list(pieces[0].shape)
    shape[axis] *= len(pieces)
    out = jax.ShapeDtypeStruct(tuple(shape), pieces[0].dtype)
    return pl.pallas_call(
        body,
        grid_spec=pltpu.PrefetchScalarGridSpec(
            num_scalar_prefetch=1,
            grid=(1,),
            in_specs=[whole(p) for p in pieces],
            out_specs=whole(out),
        ),
        out_shape=out,
        cost_estimate=FREE,
    )(here.reshape(1), *pieces)


TOP = 220.0


def products_for_partner(z, early, late, cotangent, weight):
    count = 4
    rows, features = cotangent.shape
    wide = weight.shape[0] // count

    def group(i, z_ref):
        step = 1 - 2 * (z_ref[0] % 2)
        return (z_ref[0] // 2 + jnp.where(i % 2 == 1, 4 + step * (2 - i), 2 - i)) % 4

    def body(z_ref, early_ref, late_ref, cotangent_ref, weight_ref, sent_ref, keys_ref):
        i = pl.program_id(0)

        @pl.when(i == 0)
        def _():
            keys_ref[...] = jnp.zeros_like(keys_ref)

        tokens = jnp.where(i < count // 2, early_ref[...], late_ref[...])
        keys_ref[...] += dot(tokens, weight_ref[...])
        place = pl.multiple_of(features + group(i, z_ref) * wide, 128)
        grads = dot_t(cotangent_ref[...], weight_ref[...]).astype(BF16)
        sent_ref[:rows, pl.ds(place, wide)] = grads

        @pl.when(i == count - 1)
        def _():
            keys = keys_ref[...]
            largest = jnp.maximum(jnp.max(jnp.abs(keys)) * 1.01, 1e-30)
            sent = jnp.full((16, features), largest, F32).astype(BF16)
            sent_ref[rows:, :features] = sent
            sent_ref[rows:, features:] = jnp.zeros((16, weight.shape[0]), BF16)
            scaled = keys * (TOP / sent[:1, :].astype(F32))
            power = scaled * scaled
            power = power * power
            power = power * power
            power = power * power
            sent_ref[:rows, :features] = jnp.where(scaled < 0, -power, power).astype(BF16)

    sent = jax.ShapeDtypeStruct((rows + 16, features + weight.shape[0]), BF16)
    return pl.pallas_call(
        body,
        grid_spec=pltpu.PrefetchScalarGridSpec(
            num_scalar_prefetch=1,
            grid=(count,),
            in_specs=[
                pl.BlockSpec((rows, wide), lambda i, z: (0, jnp.minimum(i, count // 2 - 1))),
                pl.BlockSpec((rows, wide), lambda i, z: (0, jnp.maximum(i - count // 2, 0))),
                whole(cotangent),
                pl.BlockSpec((wide, features), lambda i, z: (group(i, z), 0)),
            ],
            out_specs=whole(sent),
            scratch_shapes=[pltpu.VMEM(cotangent.shape, F32)],
        ),
        out_shape=sent,
        cost_estimate=FREE,
    )(z.reshape(1), early, late, cotangent, weight)


def products_here(x, tokens, cotangent, weight):
    count = 4
    rows = cotangent.shape[0]
    wide = weight.shape[0] // count

    def body(_, tokens_ref, cotangent_ref, weight_ref, keys_ref, grads_ref):
        @pl.when(pl.program_id(0) == 0)
        def _():
            keys_ref[...] = jnp.zeros_like(keys_ref)

        keys_ref[...] += dot(tokens_ref[...], weight_ref[...])
        grads_ref[...] = dot_t(cotangent_ref[...], weight_ref[...]).astype(BF16)

    here = pl.BlockSpec((rows, wide), lambda i, x: (0, x[0] * count + i))
    return pl.pallas_call(
        body,
        grid_spec=pltpu.PrefetchScalarGridSpec(
            num_scalar_prefetch=1,
            grid=(count,),
            in_specs=[
                here,
                whole(cotangent),
                pl.BlockSpec((wide, weight.shape[1]), lambda i, x: (i, 0)),
            ],
            out_specs=[whole(cotangent), here],
        ),
        out_shape=[
            jax.ShapeDtypeStruct(cotangent.shape, F32),
            jax.ShapeDtypeStruct(tokens.shape, BF16),
        ],
        cost_estimate=FREE,
    )(x.reshape(1), tokens, cotangent, weight)


def finish(x, keys, grads, back):
    count = 5
    rows, features = keys.shape
    wide = grads.shape[1] // (2 * count)

    def body(_, __, keys_ref, coded_ref, back_ref, out_ref, grads_ref):
        @pl.when(pl.program_id(0) == 0)
        def _():
            power = coded_ref[:rows, :].astype(F32)
            size = jnp.exp2(jnp.log2(jnp.abs(power)) * (1.0 / 16.0))
            size = jnp.where(power == 0, 0.0, size) * (coded_ref[rows:, :].astype(F32)[:1] / TOP)
            out_ref[...] = (keys_ref[...] + jnp.where(power < 0, -size, size)).astype(BF16)

        grads_ref[...] = back_ref[...]

    return pl.pallas_call(
        body,
        grid_spec=pltpu.PrefetchScalarGridSpec(
            num_scalar_prefetch=1,
            grid=(count,),
            in_specs=[
                pl.BlockSpec(memory_space=pl.ANY),
                whole(keys),
                pl.BlockSpec((rows + 16, features), lambda i, x: (0, 0)),
                pl.BlockSpec((rows, wide), lambda i, x: (0, features // wide + i)),
            ],
            out_specs=[
                whole(keys),
                pl.BlockSpec((rows, wide), lambda i, x: (0, (1 - x[0]) * count + i)),
            ],
        ),
        out_shape=[
            jax.ShapeDtypeStruct(keys.shape, BF16),
            jax.ShapeDtypeStruct(grads.shape, BF16),
        ],
        input_output_aliases={1: 1},
        cost_estimate=FREE,
    )(x.reshape(1), grads, keys, back, back)


def shards(activations, key_weights, key_cotangent, fragment, pseudo_grads, momentum):
    tokens, weight, cotangent, pseudo = (
        a[0] for a in (activations, key_weights, key_cotangent, pseudo_grads)
    )
    y, xh, c, x, z = (lax.axis_index(a) for a in SIZES)
    order = Sequence()
    half = tokens.shape[1] // 2
    rows = pseudo.shape[0] // 2
    mine, theirs = c * rows, (1 - c) * rows
    width = momentum.shape[1]
    pair = 2 * width
    quarter = 2 * pair
    chunk = half // N_Z
    odd_z = z % 2
    sign = 1 - 2 * odd_z
    group = z // 2
    early = [(group + 2) % 4, (group + 4 + sign) % 4]
    late = [group, (group + 4 - sign) % 4]

    def token_columns(array, side, groups):
        parts = [columns_of(array, side * half + g * 2 * chunk, 2 * chunk) for g in groups]
        return jnp.concatenate(parts, axis=1)

    weight_half = lax.all_gather(weight, "z", axis=0, tiled=True)
    cotangent_other = swap(cotangent, "xl")

    give = rows_of(pseudo, theirs, rows)
    order.did(give)
    pseudo_other = swap(give, "c")
    peaks = local_peaks(order.step(tokens), cotangent)
    order.did(peaks)
    peaks_other = swap(peaks, "xl")
    sent = token_columns(order.step(tokens), 1 - x, early)
    order.did(sent)
    early_other = swap(sent, "xl")
    pseudo_other = order.step(pseudo_other)
    total = rows_of(pseudo, mine, rows) + pseudo_other
    gives = [columns_of(total, (y ^ m) * quarter, quarter) for m in (1, 2, 3)]
    old_give = rows_of(momentum, theirs, rows)
    order.did(*gives, old_give)
    others = [swap(g, "y", m) for g, m in zip(gives, (1, 2, 3))]
    old_other = swap(old_give, "c")
    sent = token_columns(order.step(tokens), 1 - x, late)
    order.did(sent)
    late_other = swap(sent, "xl")
    peaks = join_peaks(peaks, order.step(peaks_other))
    order.did(peaks)
    peaks_other = swap(peaks, "z", 1)
    early_mine = token_columns(order.step(tokens), x, early)
    order.did(early_mine)
    peaks = join_peaks(peaks, order.step(peaks_other))
    order.did(peaks)
    peaks_other = swap(peaks, "z", 2)
    *others, old_other = order.step(*others, old_other)
    summed = columns_of(total, y * quarter, quarter) + others[0] + others[1] + others[2]
    give = columns_of(summed, (1 - xh) * pair, pair)
    order.did(summed, give)
    summed_other = swap(give, "xh")
    peaks = join_peaks(peaks, order.step(peaks_other))
    order.did(peaks)
    peaks_other = swap(peaks, "z", 4)

    def product(first, second):
        return lax.dot_general(
            jnp.concatenate([first, second], axis=0),
            jnp.concatenate([cotangent, cotangent_other], axis=0),
            (((0,), (0,)), ((), ())),
            preferred_element_type=F32,
        )

    early_other, cotangent_other = order.step(early_other, cotangent_other)
    partial_early = product(early_mine, early_other)
    order.did(partial_early)
    peaks = join_peaks(peaks, order.step(peaks_other))
    bound = jnp.maximum(peaks[0, 0] * peaks[4, 0], 1e-32)
    scale, back = 240.0 / bound, bound / (64.0 * 240.0)
    place = {4: odd_z, -3: 1 - odd_z, 2: 2 + odd_z, 3: 3 - odd_z}
    place_late = {0: odd_z, 1: 1 - odd_z, -2: 2 + odd_z, -1: 3 - odd_z}

    def own(distance, start=0, size=chunk):
        if distance in place:
            return rows_of(partial_early, place[distance] * chunk + start, size) * scale
        return rows_of(partial_late, place_late[distance] * chunk + start, size) * scale

    def send(value, pairs):
        message = encode(value)
        order.did(message)
        return lax.ppermute(message, "z", pairs)

    def ring_step(distance, even_in, odd_in):
        odd_out = send(own(-distance) + decode(order.step(even_in)), ODD)
        even_out = send(own(distance) + decode(order.step(odd_in)), EVEN)
        return even_out, odd_out

    part = chunk // 2
    far_even = send(own(4, 0, part), EVEN)
    far_odd = send(own(4, part, part), ODD)

    late_other = order.step(late_other)
    late_mine = token_columns(tokens, x, late)
    partial_late = product(late_mine, late_other)
    order.did(partial_late)

    summed_other = order.step(summed_other)
    average = (columns_of(summed, xh * pair, pair) + summed_other) / 16
    old = in_order(c, rows_of(momentum, mine, rows), old_other, 1)
    new = NESTEROV * old + average
    here = lax.dynamic_slice(fragment, (mine, (2 * y + xh) * pair), (rows, pair))
    updated = (here.astype(F32) - OUTER_RATE * (average + NESTEROV * new)).astype(BF16)
    keep = jnp.where(c == 0, new[:, :width], new[:, width:])
    give = jnp.where(c == 0, new[:, width:], new[:, :width])
    order.did(updated, keep, give)
    updated_other = swap(updated, "xh")
    new_other = swap(give, "c")

    updated_other = order.step(updated_other)
    wide = assemble(xh, lambda i: (i, 1 - i), (updated, updated_other), 1)
    order.did(wide)
    wides = [swap(wide, "y", m) for m in (1, 2, 3)]

    far_even, far_odd = order.step(far_even, far_odd)
    odd = jnp.concatenate([own(-3, 0, part) + decode(far_even), own(-3, part, part)])
    odd = send(odd, ODD)
    even = jnp.concatenate([own(3, 0, part), own(3, part, part) + decode(far_odd)])
    even = send(even, EVEN)

    weight_half = order.step(weight_half)
    sent = products_for_partner(z, early_other, late_other, cotangent_other, weight_half)
    order.did(sent)
    products_back = swap(sent, "xl")

    wides = order.step(*wides)
    block = assemble(y, lambda i: (i, i ^ 1, i ^ 2, i ^ 3), (wide, *wides), 1)
    order.did(block)
    block_other = swap(block, "c")

    even, odd = ring_step(2, even, odd)

    keys_mine, grads_mine = products_here(order.step(x), tokens, cotangent, weight_half)
    order.did(keys_mine, grads_mine)
    new_momentum = assemble(c, lambda i: (i, 1 - i), (keep, order.step(new_other)), 0)
    order.did(new_momentum)
    new_fragment = assemble(c, lambda i: (i, 1 - i), (block, order.step(block_other)), 0)
    order.did(new_fragment)

    even, odd = order.step(even, odd)
    even, odd = encode(own(1) + decode(odd)), encode(own(-1) + decode(even))
    order.did(even, odd)
    even, odd = lax.ppermute(even, "z", EVEN), lax.ppermute(odd, "z", ODD)

    products_back = order.step(products_back)
    key_out, act_grad = finish(x, keys_mine, grads_mine, products_back)
    order.did(key_out, act_grad)
    even, odd = order.step(even, odd)
    weight_grad = ((own(0) + decode(even) + decode(odd)) * back).astype(BF16)
    order.did(weight_grad)
    return (
        key_out[None],
        act_grad[None],
        weight_grad[None],
        new_fragment,
        new_momentum,
    )


def solution(mesh):
    fine = Mesh(mesh.devices.reshape(tuple(SIZES.values())), tuple(SIZES))
    return jax.shard_map(
        shards,
        mesh=fine,
        in_specs=(
            P(REP, FSDP, None),
            P(REP, FSDP, None),
            P(REP, FSDP, None),
            P(FSDP, None),
            P(REP, FSDP, None),
            P(FSDP, REP),
        ),
        out_specs=(
            P(REP, FSDP, None),
            P(REP, FSDP, None),
            P(REP, FSDP, None),
            P(FSDP, None),
            P(FSDP, REP),
        ),
        check_vma=False,
    )
```

```python
import jax
import jax.numpy as jnp
from jax import lax
from jax.experimental import pallas as pl
from jax.experimental.pallas import tpu as pltpu
from jax.sharding import Mesh
from jax.sharding import PartitionSpec as P

OUTER_RATE = 0.7
NESTEROV = 0.9
BF16 = jnp.bfloat16
F32 = jnp.float32
F16 = jnp.float16

SIZES = {"y": 4, "xh": 2, "c": 2, "xl": 2, "z": 8}
REP = ("y", "xh", "c")
FSDP = ("xl", "z")
N_Z = 8
EVEN = [(i, i ^ 1) for i in range(N_Z)]
ODD = [(i, (i - 1) % N_Z if i % 2 == 0 else (i + 1) % N_Z) for i in range(N_Z)]


def swap(value, axis, mask=1):
    return lax.ppermute(value, axis, [(i, i ^ mask) for i in range(SIZES[axis])])


class Sequence:
    def __init__(self):
        self.last = ()

    def step(self, *values):
        held = lax.optimization_barrier((*values, *self.last))[: len(values)]
        return held[0] if len(held) == 1 else held

    def did(self, *values):
        self.last = values


def rows_of(array, start, size):
    return lax.dynamic_slice_in_dim(array, start, size, 0)


def columns_of(array, start, size):
    return lax.dynamic_slice_in_dim(array, start, size, 1)


def in_order(here, mine, theirs, axis):
    first = here == 0
    return jnp.concatenate(
        [jnp.where(first, mine, theirs), jnp.where(first, theirs, mine)], axis=axis
    )


def encode(scaled):
    return (scaled * jnp.abs(scaled)).astype(F16)


def decode(sent):
    wide = sent.astype(F32)
    return jnp.sign(wide) * jnp.sqrt(jnp.abs(wide))


def tile_rows():
    return lax.broadcasted_iota(jnp.int32, (8, 128), 0)


def local_peaks(tokens, cotangent):
    peak = jnp.max(jnp.sum(jnp.abs(tokens.astype(F32)), axis=0))
    return jnp.where(tile_rows() < 4, peak, jnp.max(jnp.abs(cotangent)).astype(F32))


def join_peaks(peaks, other):
    return jnp.where(tile_rows() < 4, peaks + other, jnp.maximum(peaks, other))


def dot(left, right):
    return jnp.dot(left, right, preferred_element_type=F32)


def dot_t(left, right):
    return lax.dot_general(left, right, (((1,), (1,)), ((), ())), preferred_element_type=F32)


FREE = pl.CostEstimate(flops=0, bytes_accessed=0, transcendentals=0)


def whole(array):
    return pl.BlockSpec(array.shape, lambda i, *_: (0, 0))


def assemble(here, places, pieces, axis):
    size = pieces[0].shape[axis]

    def body(here_ref, *refs):
        out_ref = refs[-1]
        for place, piece_ref in zip(places(here_ref[0]), refs[:-1]):
            at = pl.ds(pl.multiple_of(place * size, 32 if axis == 0 else 128), size)
            if axis == 0:
                out_ref[at, :] = piece_ref[...]
            else:
                out_ref[:, at] = piece_ref[...]

    shape = list(pieces[0].shape)
    shape[axis] *= len(pieces)
    out = jax.ShapeDtypeStruct(tuple(shape), pieces[0].dtype)
    return pl.pallas_call(
        body,
        grid_spec=pltpu.PrefetchScalarGridSpec(
            num_scalar_prefetch=1,
            grid=(1,),
            in_specs=[whole(p) for p in pieces],
            out_specs=whole(out),
        ),
        out_shape=out,
        cost_estimate=FREE,
    )(here.reshape(1), *pieces)


TOP = 220.0


def products_for_partner(z, early, late, cotangent, weight):
    count = 4
    rows, features = cotangent.shape
    wide = weight.shape[0] // count

    def group(i, z_ref):
        step = 1 - 2 * (z_ref[0] % 2)
        return (z_ref[0] // 2 + jnp.where(i % 2 == 1, 4 + step * (2 - i), 2 - i)) % 4

    def body(z_ref, early_ref, late_ref, cotangent_ref, weight_ref, sent_ref, keys_ref):
        i = pl.program_id(0)

        @pl.when(i == 0)
        def _():
            keys_ref[...] = jnp.zeros_like(keys_ref)

        tokens = jnp.where(i < count // 2, early_ref[...], late_ref[...])
        keys_ref[...] += dot(tokens, weight_ref[...])
        place = pl.multiple_of(features + group(i, z_ref) * wide, 128)
        grads = dot_t(cotangent_ref[...], weight_ref[...]).astype(BF16)
        sent_ref[:rows, pl.ds(place, wide)] = grads

        @pl.when(i == count - 1)
        def _():
            keys = keys_ref[...]
            largest = jnp.maximum(jnp.max(jnp.abs(keys)) * 1.01, 1e-30)
            sent = jnp.full((16, features), largest, F32).astype(BF16)
            sent_ref[rows:, :features] = sent
            sent_ref[rows:, features:] = jnp.zeros((16, weight.shape[0]), BF16)
            scaled = keys * (TOP / sent[:1, :].astype(F32))
            power = scaled * scaled
            power = power * power
            power = power * power
            power = power * power
            sent_ref[:rows, :features] = jnp.where(scaled < 0, -power, power).astype(BF16)

    sent = jax.ShapeDtypeStruct((rows + 16, features + weight.shape[0]), BF16)
    return pl.pallas_call(
        body,
        grid_spec=pltpu.PrefetchScalarGridSpec(
            num_scalar_prefetch=1,
            grid=(count,),
            in_specs=[
                pl.BlockSpec((rows, wide), lambda i, z: (0, jnp.minimum(i, count // 2 - 1))),
                pl.BlockSpec((rows, wide), lambda i, z: (0, jnp.maximum(i - count // 2, 0))),
                whole(cotangent),
                pl.BlockSpec((wide, features), lambda i, z: (group(i, z), 0)),
            ],
            out_specs=whole(sent),
            scratch_shapes=[pltpu.VMEM(cotangent.shape, F32)],
        ),
        out_shape=sent,
        cost_estimate=FREE,
    )(z.reshape(1), early, late, cotangent, weight)


def products_here(x, tokens, cotangent, weight):
    count = 4
    rows = cotangent.shape[0]
    wide = weight.shape[0] // count

    def body(_, tokens_ref, cotangent_ref, weight_ref, keys_ref, grads_ref):
        @pl.when(pl.program_id(0) == 0)
        def _():
            keys_ref[...] = jnp.zeros_like(keys_ref)

        keys_ref[...] += dot(tokens_ref[...], weight_ref[...])
        grads_ref[...] = dot_t(cotangent_ref[...], weight_ref[...]).astype(BF16)

    here = pl.BlockSpec((rows, wide), lambda i, x: (0, x[0] * count + i))
    return pl.pallas_call(
        body,
        grid_spec=pltpu.PrefetchScalarGridSpec(
            num_scalar_prefetch=1,
            grid=(count,),
            in_specs=[
                here,
                whole(cotangent),
                pl.BlockSpec((wide, weight.shape[1]), lambda i, x: (i, 0)),
            ],
            out_specs=[whole(cotangent), here],
        ),
        out_shape=[
            jax.ShapeDtypeStruct(cotangent.shape, F32),
            jax.ShapeDtypeStruct(tokens.shape, BF16),
        ],
        cost_estimate=FREE,
    )(x.reshape(1), tokens, cotangent, weight)


def finish(x, keys, grads, back):
    count = 5
    rows, features = keys.shape
    wide = grads.shape[1] // (2 * count)

    def body(_, __, keys_ref, coded_ref, back_ref, out_ref, grads_ref):
        @pl.when(pl.program_id(0) == 0)
        def _():
            power = coded_ref[:rows, :].astype(F32)
            size = jnp.exp2(jnp.log2(jnp.abs(power)) * (1.0 / 16.0))
            size = jnp.where(power == 0, 0.0, size) * (coded_ref[rows:, :].astype(F32)[:1] / TOP)
            out_ref[...] = (keys_ref[...] + jnp.where(power < 0, -size, size)).astype(BF16)

        grads_ref[...] = back_ref[...]

    return pl.pallas_call(
        body,
        grid_spec=pltpu.PrefetchScalarGridSpec(
            num_scalar_prefetch=1,
            grid=(count,),
            in_specs=[
                pl.BlockSpec(memory_space=pl.ANY),
                whole(keys),
                pl.BlockSpec((rows + 16, features), lambda i, x: (0, 0)),
                pl.BlockSpec((rows, wide), lambda i, x: (0, features // wide + i)),
            ],
            out_specs=[
                whole(keys),
                pl.BlockSpec((rows, wide), lambda i, x: (0, (1 - x[0]) * count + i)),
            ],
        ),
        out_shape=[
            jax.ShapeDtypeStruct(keys.shape, BF16),
            jax.ShapeDtypeStruct(grads.shape, BF16),
        ],
        input_output_aliases={1: 1},
        cost_estimate=FREE,
    )(x.reshape(1), grads, keys, back, back)


def shards(activations, key_weights, key_cotangent, fragment, pseudo_grads, momentum):
    tokens, weight, cotangent, pseudo = (
        a[0] for a in (activations, key_weights, key_cotangent, pseudo_grads)
    )
    y, xh, c, x, z = (lax.axis_index(a) for a in SIZES)
    order = Sequence()
    half = tokens.shape[1] // 2
    rows = pseudo.shape[0] // 2
    mine, theirs = c * rows, (1 - c) * rows
    width = momentum.shape[1]
    pair = 2 * width
    quarter = 2 * pair
    chunk = half // N_Z
    odd_z = z % 2
    sign = 1 - 2 * odd_z
    group = z // 2
    early = [(group + 2) % 4, (group + 4 + sign) % 4]
    late = [group, (group + 4 - sign) % 4]

    def token_columns(array, side, groups):
        parts = [columns_of(array, side * half + g * 2 * chunk, 2 * chunk) for g in groups]
        return jnp.concatenate(parts, axis=1)

    weight_half = lax.all_gather(weight, "z", axis=0, tiled=True)
    cotangent_other = swap(cotangent, "xl")

    give = rows_of(pseudo, theirs, rows)
    order.did(give)
    pseudo_other = swap(give, "c")
    peaks = local_peaks(order.step(tokens), cotangent)
    order.did(peaks)
    peaks_other = swap(peaks, "xl")
    sent = token_columns(order.step(tokens), 1 - x, early)
    order.did(sent)
    early_other = swap(sent, "xl")
    pseudo_other = order.step(pseudo_other)
    total = rows_of(pseudo, mine, rows) + pseudo_other
    gives = [columns_of(total, (y ^ m) * quarter, quarter) for m in (1, 2, 3)]
    old_give = rows_of(momentum, theirs, rows)
    order.did(*gives, old_give)
    others = [swap(g, "y", m) for g, m in zip(gives, (1, 2, 3))]
    old_other = swap(old_give, "c")
    sent = token_columns(order.step(tokens), 1 - x, late)
    order.did(sent)
    late_other = swap(sent, "xl")
    peaks = join_peaks(peaks, order.step(peaks_other))
    order.did(peaks)
    peaks_other = swap(peaks, "z", 1)
    early_mine = token_columns(order.step(tokens), x, early)
    order.did(early_mine)
    peaks = join_peaks(peaks, order.step(peaks_other))
    order.did(peaks)
    peaks_other = swap(peaks, "z", 2)
    *others, old_other = order.step(*others, old_other)
    summed = columns_of(total, y * quarter, quarter) + others[0] + others[1] + others[2]
    give = columns_of(summed, (1 - xh) * pair, pair)
    order.did(summed, give)
    summed_other = swap(give, "xh")
    peaks = join_peaks(peaks, order.step(peaks_other))
    order.did(peaks)
    peaks_other = swap(peaks, "z", 4)

    def product(first, second):
        return lax.dot_general(
            jnp.concatenate([first, second], axis=0),
            jnp.concatenate([cotangent, cotangent_other], axis=0),
            (((0,), (0,)), ((), ())),
            preferred_element_type=F32,
        )

    early_other, cotangent_other = order.step(early_other, cotangent_other)
    partial_early = product(early_mine, early_other)
    order.did(partial_early)
    peaks = join_peaks(peaks, order.step(peaks_other))
    bound = jnp.maximum(peaks[0, 0] * peaks[4, 0], 1e-32)
    scale, back = 240.0 / bound, bound / (64.0 * 240.0)
    place = {4: odd_z, -3: 1 - odd_z, 2: 2 + odd_z, 3: 3 - odd_z}
    place_late = {0: odd_z, 1: 1 - odd_z, -2: 2 + odd_z, -1: 3 - odd_z}

    def own(distance, start=0, size=chunk):
        if distance in place:
            return rows_of(partial_early, place[distance] * chunk + start, size) * scale
        return rows_of(partial_late, place_late[distance] * chunk + start, size) * scale

    def send(value, pairs):
        message = encode(value)
        order.did(message)
        return lax.ppermute(message, "z", pairs)

    def ring_step(distance, even_in, odd_in):
        odd_out = send(own(-distance) + decode(order.step(even_in)), ODD)
        even_out = send(own(distance) + decode(order.step(odd_in)), EVEN)
        return even_out, odd_out

    part = chunk // 2
    far_even = send(own(4, 0, part), EVEN)
    far_odd = send(own(4, part, part), ODD)

    late_other = order.step(late_other)
    late_mine = token_columns(tokens, x, late)
    partial_late = product(late_mine, late_other)
    order.did(partial_late)

    summed_other = order.step(summed_other)
    average = (columns_of(summed, xh * pair, pair) + summed_other) / 16
    old = in_order(c, rows_of(momentum, mine, rows), old_other, 1)
    new = NESTEROV * old + average
    here = lax.dynamic_slice(fragment, (mine, (2 * y + xh) * pair), (rows, pair))
    updated = (here.astype(F32) - OUTER_RATE * (average + NESTEROV * new)).astype(BF16)
    keep = jnp.where(c == 0, new[:, :width], new[:, width:])
    give = jnp.where(c == 0, new[:, width:], new[:, :width])
    order.did(updated, keep, give)
    updated_other = swap(updated, "xh")
    new_other = swap(give, "c")

    updated_other = order.step(updated_other)
    wide = assemble(xh, lambda i: (i, 1 - i), (updated, updated_other), 1)
    order.did(wide)
    wides = [swap(wide, "y", m) for m in (1, 2, 3)]

    far_even, far_odd = order.step(far_even, far_odd)
    odd = jnp.concatenate([own(-3, 0, part) + decode(far_even), own(-3, part, part)])
    odd = send(odd, ODD)
    even = jnp.concatenate([own(3, 0, part), own(3, part, part) + decode(far_odd)])
    even = send(even, EVEN)

    weight_half = order.step(weight_half)
    sent = products_for_partner(z, early_other, late_other, cotangent_other, weight_half)
    order.did(sent)
    products_back = swap(sent, "xl")

    even, odd = ring_step(2, even, odd)

    wides = order.step(*wides)
    block = assemble(y, lambda i: (i, i ^ 1, i ^ 2, i ^ 3), (wide, *wides), 1)
    order.did(block)
    block_other = swap(block, "c")

    new_momentum = assemble(c, lambda i: (i, 1 - i), (keep, order.step(new_other)), 0)
    order.did(new_momentum)
    new_fragment = assemble(c, lambda i: (i, 1 - i), (block, order.step(block_other)), 0)
    order.did(new_fragment)

    even, odd = order.step(even, odd)
    even, odd = encode(own(1) + decode(odd)), encode(own(-1) + decode(even))
    order.did(even, odd)
    even, odd = lax.ppermute(even, "z", EVEN), lax.ppermute(odd, "z", ODD)

    keys_mine, grads_mine = products_here(order.step(x), tokens, cotangent, weight_half)
    order.did(keys_mine, grads_mine)
    products_back = order.step(products_back)
    key_out, act_grad = finish(x, keys_mine, grads_mine, products_back)
    order.did(key_out, act_grad)
    even, odd = order.step(even, odd)
    weight_grad = ((own(0) + decode(even) + decode(odd)) * back).astype(BF16)
    order.did(weight_grad)
    return (
        key_out[None],
        act_grad[None],
        weight_grad[None],
        new_fragment,
        new_momentum,
    )


def solution(mesh):
    fine = Mesh(mesh.devices.reshape(tuple(SIZES.values())), tuple(SIZES))
    return jax.shard_map(
        shards,
        mesh=fine,
        in_specs=(
            P(REP, FSDP, None),
            P(REP, FSDP, None),
            P(REP, FSDP, None),
            P(FSDP, None),
            P(REP, FSDP, None),
            P(FSDP, REP),
        ),
        out_specs=(
            P(REP, FSDP, None),
            P(REP, FSDP, None),
            P(REP, FSDP, None),
            P(FSDP, None),
            P(FSDP, REP),
        ),
        check_vma=False,
    )
```

```python
import jax
import jax.numpy as jnp
from jax import lax
from jax.experimental import pallas as pl
from jax.experimental.pallas import tpu as pltpu
from jax.sharding import Mesh
from jax.sharding import PartitionSpec as P

OUTER_RATE = 0.7
NESTEROV = 0.9
BF16 = jnp.bfloat16
F32 = jnp.float32
F16 = jnp.float16

SIZES = {"y": 4, "xh": 2, "c": 2, "xl": 2, "z": 8}
REP = ("y", "xh", "c")
FSDP = ("xl", "z")
N_Z = 8
EVEN = [(i, i ^ 1) for i in range(N_Z)]
ODD = [(i, (i - 1) % N_Z if i % 2 == 0 else (i + 1) % N_Z) for i in range(N_Z)]


def swap(value, axis, mask=1):
    return lax.ppermute(value, axis, [(i, i ^ mask) for i in range(SIZES[axis])])


class Sequence:
    def __init__(self):
        self.last = ()

    def step(self, *values):
        held = lax.optimization_barrier((*values, *self.last))[: len(values)]
        return held[0] if len(held) == 1 else held

    def did(self, *values):
        self.last = values


def rows_of(array, start, size):
    return lax.dynamic_slice_in_dim(array, start, size, 0)


def columns_of(array, start, size):
    return lax.dynamic_slice_in_dim(array, start, size, 1)


def in_order(here, mine, theirs, axis):
    first = here == 0
    return jnp.concatenate(
        [jnp.where(first, mine, theirs), jnp.where(first, theirs, mine)], axis=axis
    )


def encode(scaled):
    return (scaled * jnp.abs(scaled)).astype(F16)


def decode(sent):
    wide = sent.astype(F32)
    return jnp.sign(wide) * jnp.sqrt(jnp.abs(wide))


def tile_rows():
    return lax.broadcasted_iota(jnp.int32, (8, 128), 0)


def local_peaks(tokens, cotangent):
    peak = jnp.max(jnp.sum(jnp.abs(tokens.astype(F32)), axis=0))
    return jnp.where(tile_rows() < 4, peak, jnp.max(jnp.abs(cotangent)).astype(F32))


def join_peaks(peaks, other):
    return jnp.where(tile_rows() < 4, peaks + other, jnp.maximum(peaks, other))


def dot(left, right):
    return jnp.dot(left, right, preferred_element_type=F32)


def dot_t(left, right):
    return lax.dot_general(left, right, (((1,), (1,)), ((), ())), preferred_element_type=F32)


FREE = pl.CostEstimate(flops=0, bytes_accessed=0, transcendentals=0)


def whole(array):
    return pl.BlockSpec(array.shape, lambda i, *_: (0, 0))


def assemble(here, places, pieces, axis):
    size = pieces[0].shape[axis]

    def body(here_ref, *refs):
        out_ref = refs[-1]
        for place, piece_ref in zip(places(here_ref[0]), refs[:-1]):
            at = pl.ds(pl.multiple_of(place * size, 32 if axis == 0 else 128), size)
            if axis == 0:
                out_ref[at, :] = piece_ref[...]
            else:
                out_ref[:, at] = piece_ref[...]

    shape = list(pieces[0].shape)
    shape[axis] *= len(pieces)
    out = jax.ShapeDtypeStruct(tuple(shape), pieces[0].dtype)
    return pl.pallas_call(
        body,
        grid_spec=pltpu.PrefetchScalarGridSpec(
            num_scalar_prefetch=1,
            grid=(1,),
            in_specs=[whole(p) for p in pieces],
            out_specs=whole(out),
        ),
        out_shape=out,
        cost_estimate=FREE,
    )(here.reshape(1), *pieces)


TOP = 220.0


def products_for_partner(z, early, late, cotangent, weight):
    count = 4
    rows, features = cotangent.shape
    total = weight.shape[0]
    wide = weight.shape[0] // count

    def group(i, z_ref):
        step = 1 - 2 * (z_ref[0] % 2)
        return (z_ref[0] // 2 + jnp.where(i % 2 == 1, 4 + step * (2 - i), 2 - i)) % 4

    def body(z_ref, early_ref, late_ref, cotangent_ref, weight_ref, sent_ref, keys_ref):
        i = pl.program_id(0)

        @pl.when(i == 0)
        def _():
            keys_ref[...] = jnp.zeros_like(keys_ref)

        tokens = jnp.where(i < count // 2, early_ref[...], late_ref[...])
        keys_ref[...] += dot(tokens, weight_ref[...])
        place = pl.multiple_of(group(i, z_ref) * wide, 128)
        grads = dot_t(cotangent_ref[...], weight_ref[...]).astype(BF16)
        sent_ref[:, pl.ds(place, wide)] = grads

        @pl.when(i == count - 1)
        def _():
            keys = keys_ref[...]
            largest = jnp.maximum(jnp.max(jnp.abs(keys)) * 1.01, 1e-30)
            sent = jnp.full((rows, 128), largest, F32).astype(BF16)
            sent_ref[:, total + features :] = sent
            scaled = keys * (TOP / sent[:, :1].astype(F32))
            power = scaled * scaled
            power = power * power
            power = power * power
            power = power * power
            sent_ref[:, total : total + features] = jnp.where(scaled < 0, -power, power).astype(BF16)

    sent = jax.ShapeDtypeStruct((rows, total + features + 128), BF16)
    return pl.pallas_call(
        body,
        grid_spec=pltpu.PrefetchScalarGridSpec(
            num_scalar_prefetch=1,
            grid=(count,),
            in_specs=[
                pl.BlockSpec((rows, wide), lambda i, z: (0, jnp.minimum(i, count // 2 - 1))),
                pl.BlockSpec((rows, wide), lambda i, z: (0, jnp.maximum(i - count // 2, 0))),
                whole(cotangent),
                pl.BlockSpec((wide, features), lambda i, z: (group(i, z), 0)),
            ],
            out_specs=whole(sent),
            scratch_shapes=[pltpu.VMEM(cotangent.shape, F32)],
        ),
        out_shape=sent,
        cost_estimate=FREE,
    )(z.reshape(1), early, late, cotangent, weight)


def products_here(x, tokens, cotangent, weight):
    count = 4
    rows = cotangent.shape[0]
    wide = weight.shape[0] // count

    def body(_, tokens_ref, cotangent_ref, weight_ref, keys_ref, grads_ref):
        @pl.when(pl.program_id(0) == 0)
        def _():
            keys_ref[...] = jnp.zeros_like(keys_ref)

        keys_ref[...] += dot(tokens_ref[...], weight_ref[...])
        grads_ref[...] = dot_t(cotangent_ref[...], weight_ref[...]).astype(BF16)

    here = pl.BlockSpec((rows, wide), lambda i, x: (0, x[0] * count + i))
    return pl.pallas_call(
        body,
        grid_spec=pltpu.PrefetchScalarGridSpec(
            num_scalar_prefetch=1,
            grid=(count,),
            in_specs=[
                here,
                whole(cotangent),
                pl.BlockSpec((wide, weight.shape[1]), lambda i, x: (i, 0)),
            ],
            out_specs=[whole(cotangent), here],
        ),
        out_shape=[
            jax.ShapeDtypeStruct(cotangent.shape, F32),
            jax.ShapeDtypeStruct(tokens.shape, BF16),
        ],
        cost_estimate=FREE,
    )(x.reshape(1), tokens, cotangent, weight)


def finish(x, keys, grads, back):
    count = 2
    rows, features = keys.shape
    total = grads.shape[1] // 2
    wide = total // count

    def body(_, __, keys_ref, low_ref, high_ref, largest_ref, back_ref, out_ref, grads_ref):
        @pl.when(pl.program_id(0) == 0)
        def _():
            power = jnp.concatenate([low_ref[...], high_ref[...]], axis=1).astype(F32)
            size = jnp.exp2(jnp.log2(jnp.abs(power)) * (1.0 / 16.0))
            size = jnp.where(power == 0, 0.0, size) * (largest_ref[...].astype(F32)[:, :1] / TOP)
            out_ref[...] = (keys_ref[...] + jnp.where(power < 0, -size, size)).astype(BF16)

        grads_ref[...] = back_ref[...]

    return pl.pallas_call(
        body,
        grid_spec=pltpu.PrefetchScalarGridSpec(
            num_scalar_prefetch=1,
            grid=(count,),
            in_specs=[
                pl.BlockSpec(memory_space=pl.ANY),
                whole(keys),
                pl.BlockSpec((rows, features // 2), lambda i, x: (0, total // (features // 2))),
                pl.BlockSpec((rows, features // 2), lambda i, x: (0, total // (features // 2) + 1)),
                pl.BlockSpec((rows, 128), lambda i, x: (0, (total + features) // 128)),
                pl.BlockSpec((rows, wide), lambda i, x: (0, i)),
            ],
            out_specs=[
                whole(keys),
                pl.BlockSpec((rows, wide), lambda i, x: (0, (1 - x[0]) * count + i)),
            ],
        ),
        out_shape=[
            jax.ShapeDtypeStruct(keys.shape, BF16),
            jax.ShapeDtypeStruct(grads.shape, BF16),
        ],
        input_output_aliases={1: 1},
        cost_estimate=FREE,
    )(x.reshape(1), grads, keys, back, back, back, back)


def shards(activations, key_weights, key_cotangent, fragment, pseudo_grads, momentum):
    tokens, weight, cotangent, pseudo = (
        a[0] for a in (activations, key_weights, key_cotangent, pseudo_grads)
    )
    y, xh, c, x, z = (lax.axis_index(a) for a in SIZES)
    order = Sequence()
    half = tokens.shape[1] // 2
    rows = pseudo.shape[0] // 2
    mine, theirs = c * rows, (1 - c) * rows
    width = momentum.shape[1]
    pair = 2 * width
    quarter = 2 * pair
    chunk = half // N_Z
    odd_z = z % 2
    sign = 1 - 2 * odd_z
    group = z // 2
    early = [(group + 2) % 4, (group + 4 + sign) % 4]
    late = [group, (group + 4 - sign) % 4]

    def token_columns(array, side, groups):
        parts = [columns_of(array, side * half + g * 2 * chunk, 2 * chunk) for g in groups]
        return jnp.concatenate(parts, axis=1)

    weight_half = lax.all_gather(weight, "z", axis=0, tiled=True)
    cotangent_other = swap(cotangent, "xl")

    give = rows_of(pseudo, theirs, rows)
    order.did(give)
    pseudo_other = swap(give, "c")
    peaks = local_peaks(order.step(tokens), cotangent)
    order.did(peaks)
    peaks_other = swap(peaks, "xl")
    sent = token_columns(order.step(tokens), 1 - x, early)
    order.did(sent)
    early_other = swap(sent, "xl")
    pseudo_other = order.step(pseudo_other)
    total = rows_of(pseudo, mine, rows) + pseudo_other
    gives = [columns_of(total, (y ^ m) * quarter, quarter) for m in (1, 2, 3)]
    old_give = rows_of(momentum, theirs, rows)
    order.did(*gives, old_give)
    others = [swap(g, "y", m) for g, m in zip(gives, (1, 2, 3))]
    old_other = swap(old_give, "c")
    sent = token_columns(order.step(tokens), 1 - x, late)
    order.did(sent)
    late_other = swap(sent, "xl")
    peaks = join_peaks(peaks, order.step(peaks_other))
    order.did(peaks)
    peaks_other = swap(peaks, "z", 1)
    early_mine = token_columns(order.step(tokens), x, early)
    order.did(early_mine)
    peaks = join_peaks(peaks, order.step(peaks_other))
    order.did(peaks)
    peaks_other = swap(peaks, "z", 2)
    *others, old_other = order.step(*others, old_other)
    summed = columns_of(total, y * quarter, quarter) + others[0] + others[1] + others[2]
    give = columns_of(summed, (1 - xh) * pair, pair)
    order.did(summed, give)
    summed_other = swap(give, "xh")
    peaks = join_peaks(peaks, order.step(peaks_other))
    order.did(peaks)
    peaks_other = swap(peaks, "z", 4)

    def product(first, second):
        return lax.dot_general(
            jnp.concatenate([first, second], axis=0),
            jnp.concatenate([cotangent, cotangent_other], axis=0),
            (((0,), (0,)), ((), ())),
            preferred_element_type=F32,
        )

    early_other, cotangent_other = order.step(early_other, cotangent_other)
    partial_early = product(early_mine, early_other)
    order.did(partial_early)
    peaks = join_peaks(peaks, order.step(peaks_other))
    bound = jnp.maximum(peaks[0, 0] * peaks[4, 0], 1e-32)
    scale, back = 240.0 / bound, bound / (64.0 * 240.0)
    place = {4: odd_z, -3: 1 - odd_z, 2: 2 + odd_z, 3: 3 - odd_z}
    place_late = {0: odd_z, 1: 1 - odd_z, -2: 2 + odd_z, -1: 3 - odd_z}

    def own(distance, start=0, size=chunk):
        if distance in place:
            return rows_of(partial_early, place[distance] * chunk + start, size) * scale
        return rows_of(partial_late, place_late[distance] * chunk + start, size) * scale

    def send(value, pairs):
        message = encode(value)
        order.did(message)
        return lax.ppermute(message, "z", pairs)

    def ring_step(distance, even_in, odd_in):
        odd_out = send(own(-distance) + decode(order.step(even_in)), ODD)
        even_out = send(own(distance) + decode(order.step(odd_in)), EVEN)
        return even_out, odd_out

    part = chunk // 2
    far_even = send(own(4, 0, part), EVEN)
    far_odd = send(own(4, part, part), ODD)

    late_other = order.step(late_other)
    late_mine = token_columns(tokens, x, late)
    partial_late = product(late_mine, late_other)
    order.did(partial_late)

    summed_other = order.step(summed_other)
    average = (columns_of(summed, xh * pair, pair) + summed_other) / 16
    old = in_order(c, rows_of(momentum, mine, rows), old_other, 1)
    new = NESTEROV * old + average
    here = lax.dynamic_slice(fragment, (mine, (2 * y + xh) * pair), (rows, pair))
    updated = (here.astype(F32) - OUTER_RATE * (average + NESTEROV * new)).astype(BF16)
    keep = jnp.where(c == 0, new[:, :width], new[:, width:])
    give = jnp.where(c == 0, new[:, width:], new[:, :width])
    order.did(updated, keep, give)
    updated_other = swap(updated, "xh")
    new_other = swap(give, "c")

    updated_other = order.step(updated_other)
    wide = assemble(xh, lambda i: (i, 1 - i), (updated, updated_other), 1)
    order.did(wide)
    wides = [swap(wide, "y", m) for m in (1, 2, 3)]

    far_even, far_odd = order.step(far_even, far_odd)
    odd = jnp.concatenate([own(-3, 0, part) + decode(far_even), own(-3, part, part)])
    odd = send(odd, ODD)
    even = jnp.concatenate([own(3, 0, part), own(3, part, part) + decode(far_odd)])
    even = send(even, EVEN)

    weight_half = order.step(weight_half)
    sent = products_for_partner(z, early_other, late_other, cotangent_other, weight_half)
    order.did(sent)
    products_back = swap(sent, "xl")

    wides = order.step(*wides)
    block = assemble(y, lambda i: (i, i ^ 1, i ^ 2, i ^ 3), (wide, *wides), 1)
    order.did(block)
    block_other = swap(block, "c")

    even, odd = ring_step(2, even, odd)

    keys_mine, grads_mine = products_here(order.step(x), tokens, cotangent, weight_half)
    order.did(keys_mine, grads_mine)
    new_momentum = assemble(c, lambda i: (i, 1 - i), (keep, order.step(new_other)), 0)
    order.did(new_momentum)
    new_fragment = assemble(c, lambda i: (i, 1 - i), (block, order.step(block_other)), 0)
    order.did(new_fragment)

    even, odd = order.step(even, odd)
    even, odd = encode(own(1) + decode(odd)), encode(own(-1) + decode(even))
    order.did(even, odd)
    even, odd = lax.ppermute(even, "z", EVEN), lax.ppermute(odd, "z", ODD)

    products_back = order.step(products_back)
    key_out, act_grad = finish(x, keys_mine, grads_mine, products_back)
    order.did(key_out, act_grad)
    even, odd = order.step(even, odd)
    weight_grad = ((own(0) + decode(even) + decode(odd)) * back).astype(BF16)
    order.did(weight_grad)
    return (
        key_out[None],
        act_grad[None],
        weight_grad[None],
        new_fragment,
        new_momentum,
    )


def solution(mesh):
    fine = Mesh(mesh.devices.reshape(tuple(SIZES.values())), tuple(SIZES))
    return jax.shard_map(
        shards,
        mesh=fine,
        in_specs=(
            P(REP, FSDP, None),
            P(REP, FSDP, None),
            P(REP, FSDP, None),
            P(FSDP, None),
            P(REP, FSDP, None),
            P(FSDP, REP),
        ),
        out_specs=(
            P(REP, FSDP, None),
            P(REP, FSDP, None),
            P(REP, FSDP, None),
            P(FSDP, None),
            P(FSDP, REP),
        ),
        check_vma=False,
    )
```
